256 devices in a mesh: lat: 16 (over z, y_lo), lon: 16 (over x, y_hi, core).
Axes of the slice: x: 4, y: 4 (y_hi: 2, y_lo: 2; y = y_hi * 2 + y_lo), z: 8, core: 2. Of those that a mesh axis runs over, the one named last changes fastest.
Arguments:
- features: bfloat16 [256, 512, 512], P('lat', 'lon'), may hold values from -6 to 6
- land_mask: int32 [256, 512], P('lat', 'lon'), may hold values 0 or 1
- land_embed: float32 [512], replicated, may hold values from -4 to 4
- window_shift: int32 [1], replicated, may hold values from 1 to 15
- fine_gain: float32 [512], replicated, may hold values from 0.5 to 1.5
- qkv_weight: bfloat16 [512, 1536], replicated, may hold values from -0.25 to 0.25
- bias_table: float32 [8, 465], replicated, may hold values from -4 to 400
- mix_weight: bfloat16 [512, 512], replicated, may hold values from -0.25 to 0.25
- merge_gain: float32 [2048], replicated, may hold values from 0.5 to 1.5
- merge_weight: bfloat16 [2048, 1024], replicated, may hold values from -0.125 to 0.125
- coarse_gain: float32 [1024], replicated, may hold values from 0.5 to 1.5
- inner_weight: bfloat16 [1024, 4096], P(None, 'lon'), may hold values from -0.1875 to 0.1875
- outer_weight: bfloat16 [4096, 1024], P('lon'), may hold values from -0.09375 to 0.09375
- expand_weight: bfloat16 [1024, 2048], replicated, may hold values from -0.1875 to 0.1875
- cotangent: bfloat16 [256, 512, 512], P('lat', 'lon'), may hold values from -0.25 to 0.25
Outputs:
- prediction: bfloat16 [256, 512, 512], P('lat', 'lon')
- grad_inner: float32 [1024, 4096], P('lat', 'lon')
- grad_outer: float32 [4096, 1024], P('lon', 'lat')
The draws below stay inside these ranges and needn't reach their ends.
All inputs are finite; a program needn't handle non-finite values. No bound on the sum of `land_mask` on one device may be relied on, other than what follows from the above.
Results may differ from the reference program's by a relative error of at most 0.03.
Values may be sent and summed in bfloat16 or wider, within the bound.
A program may use at most 128 MiB of HBM per device.

```python
import jax
import jax.numpy as jnp
from jax import lax

D1 = 512
D2 = 1024
HEADS1 = 8
FF2 = 4096
WH = 8
WL = 16
LAT = 256
LON = 512
CTOK = 32768
NB = 465


def draw_bias_table(key, part):
    key = jax.random.fold_in(key, 11)
    return jnp.clip(jax.random.normal(key, (HEADS1, NB), jnp.float32), -4.0, 4.0)


def set_ends(entries, own_key, smallest, largest):
    dims = entries.shape
    spot = [jax.random.randint(jax.random.fold_in(own_key, axis), (), 0, dims[axis]) for axis in range(len(dims))]
    entries = entries.at[tuple(spot)].set(smallest)
    longest = dims.index(max(dims))
    spot[longest] = (spot[longest] + 1) % dims[longest]
    return entries.at[tuple(spot)].set(largest)


def steps_of(stream_key, dims, cuts, least, high):
    def one(position, shards_of):
        steps = jax.random.uniform(jax.random.fold_in(jax.random.fold_in(stream_key, 6), position), (shards_of,), jnp.float32, least / len(cuts), high / len(cuts))
        return jnp.repeat(jnp.exp(steps), dims[position] // shards_of).reshape((-1,) + (1,) * (len(dims) - position - 1))

    level = one(*cuts[0])
    for cut in cuts[1:]:
        level = level * one(*cut)
    return level


def scatter_about(rng, shape, scale, limit, pieces=(), kind=jnp.bfloat16):
    level = steps_of(rng, shape, pieces, -0.22, 0.18) if pieces else 1.0
    array = jax.random.normal(rng, shape, jnp.float32) * scale * level
    return jnp.minimum(jnp.maximum(array, -limit), limit).astype(kind)


def setup_inputs(seed: int = 0) -> dict:
    keys = jax.random.split(jax.random.key(seed), 16)
    return {
        "features": scatter_about(keys[0], (LAT, LON, D1), 1.0, 6.0, ((0, 16), (1, 16))),
        "land_mask": set_ends((jax.random.randint(keys[1], (LAT, LON), 0, 3) < 1).astype(jnp.int32), jax.random.fold_in(keys[1], 1), 0, 1),
        "land_embed": scatter_about(keys[2], (D1,), 1.0, 4.0, (), jnp.float32),
        "window_shift": jax.random.randint(keys[3], (1,), 1, WL).astype(jnp.int32),
        "fine_gain": jnp.clip(1.0 + 0.1 * jax.random.normal(keys[4], (D1,), jnp.float32), 0.5, 1.5),
        "qkv_weight": scatter_about(keys[5], (D1, 3 * D1), D1 ** -0.5, 0.25),
        "bias_table": draw_bias_table(jax.random.fold_in(keys[15], 71), 0),
        "mix_weight": scatter_about(keys[7], (D1, D1), D1 ** -0.5, 0.25),
        "merge_gain": jnp.clip(1.0 + 0.1 * jax.random.normal(keys[8], (4 * D1,), jnp.float32), 0.5, 1.5),
        "merge_weight": scatter_about(keys[9], (4 * D1, D2), (4 * D1) ** -0.5, 0.125),
        "coarse_gain": jnp.clip(1.0 + 0.1 * jax.random.normal(keys[10], (D2,), jnp.float32), 0.5, 1.5),
        "inner_weight": scatter_about(keys[11], (D2, FF2), D2 ** -0.5, 0.1875, ((1, 16),)),
        "outer_weight": scatter_about(keys[12], (FF2, D2), FF2 ** -0.5, 0.09375, ((0, 16),)),
        "expand_weight": scatter_about(keys[13], (D2, 4 * D1), D2 ** -0.5, 0.1875),
        "cotangent": scatter_about(keys[14], (LAT, LON, D1), (8.0 / CTOK ** 0.5), 0.25, ((0, 16), (1, 16))),
    }


NORM_EPS = 1e-05
GELU_SCALE = 0.7978845608028654

def layer_norm(values, gain):
    centre = lax.optimization_barrier(jnp.mean(values, axis=-1, keepdims=True))
    centred = values - centre
    spread = lax.optimization_barrier(jnp.mean(centred * centred, axis=-1, keepdims=True))
    return centred * lax.rsqrt(spread + NORM_EPS) * gain

def gelu_pair(pre_act):
    inner = GELU_SCALE * (pre_act + 0.044715 * pre_act * pre_act * pre_act)
    tangent = jnp.tanh(inner)
    value = 0.5 * pre_act * (1.0 + tangent)
    slope = 0.5 * (1.0 + tangent) + 0.5 * pre_act * (1.0 - tangent * tangent) * GELU_SCALE * (1.0 + 3.0 * 0.044715 * pre_act * pre_act)
    return (value, slope)

def bias_matrix(bias_table, win_rows, win_cols):
    places = jnp.arange(win_rows * win_cols, dtype=jnp.int32)
    place_row = places // win_cols
    place_col = places % win_cols
    lookup = (place_row[:, None] - place_row[None, :] + win_rows - 1) * (2 * win_cols - 1) + (place_col[:, None] - place_col[None, :] + win_cols - 1)
    return bias_table[:, lookup]

def window_attention(normed, qkv_weight, position_bias, win_rows, win_cols, head_count):
    grid_rows, grid_cols, feat_width = normed.shape
    window_size = win_rows * win_cols
    head_size = feat_width // head_count
    windows = normed.reshape(grid_rows // win_rows, win_rows, grid_cols // win_cols, win_cols, feat_width)
    windows = windows.transpose(0, 2, 1, 3, 4).reshape(-1, window_size, feat_width)
    projected = jnp.dot(windows, qkv_weight, preferred_element_type=jnp.float32).astype(jnp.bfloat16)
    projected = projected.reshape(windows.shape[0], window_size, 3, head_count, head_size)
    queries = projected[:, :, 0].astype(jnp.float32)
    key_rows = projected[:, :, 1].astype(jnp.float32)
    values = projected[:, :, 2].astype(jnp.float32)
    scores = jnp.einsum('nqhd,nkhd->nhqk', queries, key_rows) * head_size ** (-0.5) + position_bias[None]
    row_max = lax.optimization_barrier(jnp.max(scores, axis=-1, keepdims=True))
    expo = jnp.exp(scores - row_max)
    prob_rows = (expo / lax.optimization_barrier(jnp.sum(expo, axis=-1, keepdims=True))).astype(jnp.bfloat16)
    attended = jnp.einsum('nhqk,nkhd->nqhd', prob_rows.astype(jnp.float32), values).astype(jnp.bfloat16)
    attended = attended.reshape(grid_rows // win_rows, grid_cols // win_cols, win_rows, win_cols, feat_width)
    return attended.transpose(0, 2, 1, 3, 4).reshape(grid_rows, grid_cols, feat_width)

def fold_quads(grid):
    grid_rows, grid_cols, feat_width = grid.shape
    folded = grid.reshape(grid_rows // 2, 2, grid_cols // 2, 2, feat_width).transpose(0, 2, 1, 3, 4)
    return folded.reshape(grid_rows // 2, grid_cols // 2, 4 * feat_width)

def unfold_quads(grid, feat_width):
    grid_rows, grid_cols, total_width = grid.shape
    spread_out = grid.reshape(grid_rows, grid_cols, 2, 2, feat_width).transpose(0, 2, 1, 3, 4)
    return spread_out.reshape(grid_rows * 2, grid_cols * 2, feat_width)

def reference(features, land_mask, land_embed, window_shift, fine_gain, qkv_weight, bias_table, mix_weight, merge_gain, merge_weight, coarse_gain, inner_weight, outer_weight, expand_weight, cotangent):
    position_bias = bias_matrix(bias_table, WH, WL)
    offset = window_shift[0]
    block_count = LAT // WH

    def block_step(running, block_index):
        grad_in, grad_out = running
        first_row = block_index * WH
        feature_rows = lax.dynamic_slice_in_dim(features, first_row, WH, 0).astype(jnp.float32)
        land_rows = lax.dynamic_slice_in_dim(land_mask, first_row, WH, 0).astype(jnp.float32)
        base_rows = feature_rows + land_rows[..., None] * land_embed
        normed = layer_norm(base_rows, fine_gain).astype(jnp.bfloat16)
        rolled = jnp.roll(normed, -offset, axis=1)
        attended = jnp.roll(window_attention(rolled, qkv_weight, position_bias, WH, WL, HEADS1), offset, axis=1)
        level_one = (base_rows + jnp.dot(attended, mix_weight, preferred_element_type=jnp.float32)).astype(jnp.bfloat16)
        merged = layer_norm(fold_quads(level_one).astype(jnp.float32), merge_gain).astype(jnp.bfloat16)
        coarse_cells = jnp.dot(merged.reshape(-1, 4 * D1), merge_weight, preferred_element_type=jnp.float32).astype(jnp.bfloat16)
        lifted = layer_norm(coarse_cells.astype(jnp.float32), coarse_gain).astype(jnp.bfloat16)
        pre_act = jnp.dot(lifted, inner_weight, preferred_element_type=jnp.float32)
        value, slope = gelu_pair(pre_act)
        hidden = value.astype(jnp.bfloat16)
        back_cells = (coarse_cells.astype(jnp.float32) + jnp.dot(hidden, outer_weight, preferred_element_type=jnp.float32)).astype(jnp.bfloat16)
        raised = jnp.dot(back_cells, expand_weight, preferred_element_type=jnp.float32).reshape(WH // 2, LON // 2, 4 * D1)
        out_block = (level_one.astype(jnp.float32) + unfold_quads(raised, D1)).astype(jnp.bfloat16)
        cot_block = lax.dynamic_slice_in_dim(cotangent, first_row, WH, 0)
        cot_folded = fold_quads(cot_block).reshape(-1, 4 * D1)
        cot_coarse = jnp.dot(cot_folded, expand_weight.T, preferred_element_type=jnp.float32).astype(jnp.bfloat16)
        cot_hidden = jnp.dot(cot_coarse, outer_weight.T, preferred_element_type=jnp.float32)
        cot_pre = (cot_hidden * slope).astype(jnp.bfloat16)
        grad_in = grad_in + jnp.dot(lifted.T, cot_pre, preferred_element_type=jnp.float32)
        grad_out = grad_out + jnp.dot(hidden.T, cot_coarse, preferred_element_type=jnp.float32)
        return ((grad_in, grad_out), out_block)
    start_grads = (jnp.zeros((D2, FF2), jnp.float32), jnp.zeros((FF2, D2), jnp.float32))
    (grad_inner, grad_outer), out_blocks = lax.scan(block_step, start_grads, jnp.arange(block_count, dtype=jnp.int32))
    prediction = out_blocks.reshape(LAT, LON, D1)
    return (prediction, grad_inner, grad_outer)
```

```python
import jax
import jax.numpy as jnp
from jax import lax
from jax.experimental import pallas as pl
from jax.experimental.pallas import tpu as pltpu
from jax.sharding import PartitionSpec as P

HEADS1 = 8
WH = 8
WL = 16


NORM_EPS = 1e-05
GELU_SCALE = 0.7978845608028654


def with_halo(cells, sides, width):
    for axis, dim in sides:
        count = lax.axis_size(axis)
        head = lax.slice_in_dim(cells, 0, width, axis=dim)
        tail = lax.slice_in_dim(cells, cells.shape[dim] - width, cells.shape[dim], axis=dim)
        cells = jnp.concatenate(
            [
                lax.ppermute(tail, axis, [(i, (i + 1) % count) for i in range(count)]),
                cells,
                lax.ppermute(head, axis, [((i + 1) % count, i) for i in range(count)]),
            ],
            axis=dim,
        )
    return cells


def layer_norm(values, gain):
    centre = jnp.mean(values, axis=-1, keepdims=True)
    centred = values - centre
    spread = jnp.mean(centred * centred, axis=-1, keepdims=True)
    return centred * lax.rsqrt(spread + NORM_EPS) * gain


def gelu_pair(pre_act):
    inner = GELU_SCALE * (pre_act + 0.044715 * pre_act * pre_act * pre_act)
    tangent = jnp.tanh(inner)
    value = 0.5 * pre_act * (1.0 + tangent)
    slope = 0.5 * (1.0 + tangent) + 0.5 * pre_act * (1.0 - tangent * tangent) * GELU_SCALE * (
        1.0 + 3.0 * 0.044715 * pre_act * pre_act
    )
    return (value, slope)


def bias_matrix(bias_table, win_rows, win_cols):
    heads = bias_table.shape[0]
    reach = 2 * win_cols - 1
    flipped = bias_table[:, ::-1].reshape(heads, 2 * win_rows - 1, reach)
    by_col = jnp.stack(
        [flipped[:, :, win_cols - 1 - j : 2 * win_cols - 1 - j] for j in range(win_cols)], axis=1
    )
    by_row = jnp.stack(
        [by_col[:, :, win_rows - 1 - i : 2 * win_rows - 1 - i] for i in range(win_rows)], axis=1
    )
    return by_row.reshape(heads, win_rows * win_cols, win_rows * win_cols)


def window_attention(normed, qkv_weight, position_bias, win_rows, win_cols, head_count):
    grid_rows, grid_cols, feat_width = normed.shape
    window_size = win_rows * win_cols
    head_size = feat_width // head_count
    windows = normed.reshape(
        grid_rows // win_rows, win_rows, grid_cols // win_cols, win_cols, feat_width
    )
    windows = windows.transpose(0, 2, 1, 3, 4).reshape(-1, window_size, feat_width)
    projected = jnp.dot(windows, qkv_weight, preferred_element_type=jnp.float32).astype(
        jnp.bfloat16
    )
    projected = projected.reshape(windows.shape[0], window_size, 3, head_count, head_size)
    queries = projected[:, :, 0]
    key_rows = projected[:, :, 1]
    values = projected[:, :, 2]
    scores = (
        jnp.einsum("nqhd,nkhd->nhqk", queries, key_rows, preferred_element_type=jnp.float32)
        * head_size ** (-0.5)
        + position_bias[None]
    )
    row_max = jnp.max(scores, axis=-1, keepdims=True)
    expo = jnp.exp(scores - row_max)
    prob_rows = (expo / jnp.sum(expo, axis=-1, keepdims=True)).astype(jnp.bfloat16)
    attended = jnp.einsum(
        "nhqk,nkhd->nqhd", prob_rows, values, preferred_element_type=jnp.float32
    ).astype(jnp.bfloat16)
    attended = attended.reshape(
        grid_rows // win_rows, grid_cols // win_cols, win_rows, win_cols, feat_width
    )
    return attended.transpose(0, 2, 1, 3, 4).reshape(grid_rows, grid_cols, feat_width)


def fold_quads(grid):
    grid_rows, grid_cols, feat_width = grid.shape
    folded = grid.reshape(grid_rows // 2, 2, grid_cols // 2, 2, feat_width).transpose(0, 2, 1, 3, 4)
    return folded.reshape(grid_rows // 2, grid_cols // 2, 4 * feat_width)


def unfold_quads(grid, feat_width):
    grid_rows, grid_cols, total_width = grid.shape
    spread_out = grid.reshape(grid_rows, grid_cols, 2, 2, feat_width).transpose(0, 2, 1, 3, 4)
    return spread_out.reshape(grid_rows * 2, grid_cols * 2, feat_width)


MESH = pl.DeviceIdType.MESH
CELLS = 128
HALF = 64


class Copies:
    def __init__(self, send_sems, recv_sems):
        self.send_sems, self.recv_sems, self.started = send_sems, recv_sems, {}

    def describe(self, name, src, dst, device):
        return pltpu.make_async_remote_copy(
            src_ref=src,
            dst_ref=dst,
            send_sem=self.send_sems.at[name],
            recv_sem=self.recv_sems.at[name],
            device_id=device,
            device_id_type=MESH,
        )

    def start(self, name, src, dst, device):
        copy = self.describe(name, src, dst, device)
        copy.start()
        self.started[name] = copy

    def arrived(self, name, dst, device):
        self.describe(name, dst, dst, device).wait_recv()

    def finish(self):
        for copy in self.started.values():
            copy.wait_send()


def exchange_kernel(
    lifted_ref, cot_ref, inner_ref, outer_ref, eye_ref,
    update_ref, grad_inner_ref, grad_outer_ref,
    lift, cots, part, core_in, half_in, full_in, pair_in,
    hidden_t, cot_pre_t, terms, ring_half, ring_full, side_out, side_in,
    send_sems, recv_sems,
):
    lon, lat = lax.axis_index("lon"), lax.axis_index("lat")
    core, y_hi, x = lon % 2, (lon // 2) % 2, lon // 4
    z, y_lo = lat // 2, lat % 2
    partner = {"lon": lon + 1 - 2 * core}
    across = {"lon": lon + 2 - 4 * y_hi}
    right, left = {"lon": (lon + 4) % 16}, {"lon": (lon + 12) % 16}
    up, down = {"lat": (lat + 2) % 16}, {"lat": (lat + 14) % 16}
    side = {"lat": lat + 1 - 2 * y_lo}

    barrier = pltpu.get_barrier_semaphore()
    neighbours = (partner, across, right, left, up, down, side)
    for device in neighbours:
        pl.semaphore_signal(barrier, inc=1, device_id=device, device_id_type=MESH)
    pl.semaphore_wait(barrier, len(neighbours))

    copies = Copies(send_sems, recv_sems)

    def chip(dx, dy):
        return ((x + dx) % 4) * 2 + (y_hi + dy) % 2

    def at(array, dx, dy, dk=0):
        return array.at[chip(dx, dy), (core + dk) % 2]

    gathers = ((0, cots, cot_ref), (20, lift, lifted_ref))
    for base, array, own in gathers:
        array[chip(0, 0), core] = own[...]
        for k, device in enumerate((partner, right, left, across)):
            copies.start(base + k, at(array, 0, 0), at(array, 0, 0), device)

    low, high = pl.ds(0, HALF), pl.ds(HALF, HALF)
    hops = ((0, (1, 2), (7, 8, 9, 10, 11)), (1, (5, 6), (12, 13, 14, 15, 16)))

    def process(dx, dy):
        p = chip(dx, dy)
        lifted = lift[p].reshape(2 * CELLS, -1)
        cot = cots[p].reshape(2 * CELLS, -1)
        pre = jnp.dot(lifted, inner_ref[...], preferred_element_type=jnp.float32)
        value, slope = gelu_pair(pre)
        hidden = value.astype(jnp.bfloat16)
        update = jnp.dot(hidden, outer_ref[...], preferred_element_type=jnp.float32)
        part[p] = update.astype(jnp.bfloat16).reshape(2, CELLS, -1)
        cot_hidden = lax.dot_general(
            cot, outer_ref[...], (((1,), (1,)), ((), ())), preferred_element_type=jnp.float32
        )
        cot_pre = (cot_hidden * slope).astype(jnp.bfloat16)
        columns = pl.ds(pl.multiple_of(p * 2 * CELLS, 2 * CELLS), 2 * CELLS)
        turn = (((1,), (1,)), ((), ()))
        hidden_t[:, columns] = lax.dot_general(
            eye_ref[...], hidden, turn, preferred_element_type=jnp.float32
        ).astype(jnp.bfloat16)
        cot_pre_t[:, columns] = lax.dot_general(
            eye_ref[...], cot_pre, turn, preferred_element_type=jnp.float32
        ).astype(jnp.bfloat16)
        name = 40 + 4 * dy + dx
        copies.start(name, part.at[p, 1 - core], core_in.at[p], partner)

    def first_hop(base, array, dy, names, forward):
        copies.arrived(base + names[0], at(array, 3, dy), right)
        copies.start(
            base + forward[0], at(array, 3, dy).at[low], at(array, 3, dy).at[low], right
        )
        copies.start(base + forward[1], at(array, 3, dy), at(array, 3, dy), partner)
        copies.arrived(base + names[1], at(array, 1, dy), left)
        copies.start(
            base + forward[2], at(array, 1, dy).at[high], at(array, 1, dy).at[high], left
        )
        copies.start(base + forward[3], at(array, 1, dy), at(array, 1, dy), partner)

    def across_hop(base, array):
        copies.arrived(base + 3, at(array, 0, 1), across)
        for k, device in ((5, right), (6, left), (4, partner)):
            copies.start(base + k, at(array, 0, 1), at(array, 0, 1), device)

    def second_hop(base, array, dy, forward):
        copies.arrived(base + forward[0], at(array, 2, dy).at[low], right)
        copies.arrived(base + forward[2], at(array, 2, dy).at[high], left)
        copies.start(base + forward[4], at(array, 2, dy), at(array, 2, dy), partner)

    def from_partner(base, array, dx, dy, name):
        copies.arrived(base + name, at(array, dx, dy, 1), partner)

    def both(step, *args):
        for base, array, own in gathers:
            step(base, array, *args)

    both(first_hop, 0, *hops[0][1:])
    both(across_hop)
    both(from_partner, 0, 0, 0)
    process(0, 0)
    both(second_hop, 0, hops[0][2])
    both(from_partner, 3, 0, 8)
    process(3, 0)
    both(from_partner, 1, 0, 10)
    process(1, 0)
    both(first_hop, 1, *hops[1][1:])
    both(from_partner, 0, 1, 4)
    process(0, 1)
    both(from_partner, 2, 0, 11)
    process(2, 0)
    both(from_partner, 3, 1, 13)
    process(3, 1)
    both(from_partner, 1, 1, 15)
    process(1, 1)
    both(second_hop, 1, hops[1][2])
    both(from_partner, 2, 1, 16)
    process(2, 1)

    def cores(dx, dy):
        p = chip(dx, dy)
        copies.arrived(40 + 4 * dy + dx, core_in.at[p], partner)
        part[p, core] = (
            part[p, core].astype(jnp.float32) + core_in[p].astype(jnp.float32)
        ).astype(jnp.bfloat16)

    def x_start(dy):
        base = 48 + 4 * dy
        cores(2, dy)
        far = at(part, 2, dy)
        copies.start(base, far.at[low], half_in.at[dy, 0], right)
        copies.start(base + 1, far.at[high], half_in.at[dy, 1], left)
        cores(1, dy)
        cores(3, dy)
        cores(0, dy)

    def x_next(dy):
        base = 48 + 4 * dy
        copies.arrived(base, half_in.at[dy, 0], right)
        p = chip(1, dy)
        part[p, core, low, :] = (
            part[p, core, low, :].astype(jnp.float32) + half_in[dy, 0].astype(jnp.float32)
        ).astype(jnp.bfloat16)
        copies.start(base + 2, part.at[p, core], full_in.at[dy, 0], right)
        copies.arrived(base + 1, half_in.at[dy, 1], left)
        p = chip(3, dy)
        part[p, core, high, :] = (
            part[p, core, high, :].astype(jnp.float32) + half_in[dy, 1].astype(jnp.float32)
        ).astype(jnp.bfloat16)
        copies.start(base + 3, part.at[p, core], full_in.at[dy, 1], left)

    def x_last(dy):
        base = 48 + 4 * dy
        copies.arrived(base + 2, full_in.at[dy, 0], right)
        copies.arrived(base + 3, full_in.at[dy, 1], left)
        return (
            part[chip(0, dy), core].astype(jnp.float32)
            + full_in[dy, 0].astype(jnp.float32)
            + full_in[dy, 1].astype(jnp.float32)
        )

    def zed(dz):
        return (z + dz) % 8

    def ring(step):
        base = 56 + 2 * step
        if step == 0:
            far = terms.at[zed(4)]
            copies.start(base, far.at[0], ring_half.at[0], up)
            copies.start(base + 1, far.at[1], ring_half.at[1], down)
            return
        for way, device, mine in ((0, up, zed(4 - step)), (1, down, zed(4 + step))):
            if step == 1:
                copies.arrived(base - 2 + way, ring_half.at[way], device)
                terms[mine, way] = (
                    terms[mine, way].astype(jnp.float32) + ring_half[way].astype(jnp.float32)
                ).astype(jnp.bfloat16)
            else:
                copies.arrived(base - 2 + way, ring_full.at[step - 2, way], device)
                terms[mine] = (
                    terms[mine].astype(jnp.float32)
                    + ring_full[step - 2, way].astype(jnp.float32)
                ).astype(jnp.bfloat16)
            copies.start(base + way, terms.at[mine], ring_full.at[step - 1, way], device)

    def ring_end():
        total = terms[z].astype(jnp.float32)
        for way, device in ((0, up), (1, down)):
            copies.arrived(62 + way, ring_full.at[2, way], device)
            total = total + ring_full[2, way].astype(jnp.float32)
        side_out[...] = jnp.stack([total[0].T, total[1].T]).reshape(2, 2, HALF, -1)
        sending = side_in.at[1]
        sending[...] = side_out[:, 1 - y_lo].astype(jnp.bfloat16)
        copies.start(64, sending, side_in.at[0], side)

    x_start(1)
    for j in range(4):
        lanes = pl.ds(j * 256, 256)
        for kind, rows, array in ((0, cot_pre_t, lift), (1, hidden_t, cots)):
            term = jnp.dot(
                rows[...],
                array[:, :, :, lanes].reshape(16 * CELLS, 256),
                preferred_element_type=jnp.float32,
            ).astype(jnp.bfloat16)
            terms[2 * j, kind] = term[:, :CELLS]
            terms[2 * j + 1, kind] = term[:, CELLS:]
    ring(0)
    x_next(1)
    x_start(0)
    ring(1)
    side_total = x_last(1)
    part[chip(0, 1), core] = side_total.astype(jnp.bfloat16)
    copies.start(65, at(part, 0, 1), pair_in, across)
    x_next(0)
    ring(2)
    ring(3)
    ring_end()
    total = x_last(0)
    copies.arrived(65, pair_in, across)
    update_ref[...] = (total + pair_in[...].astype(jnp.float32)).astype(jnp.bfloat16)
    copies.arrived(64, side_in.at[0], side)
    final = side_out[:, y_lo] + side_in[0].astype(jnp.float32)
    grad_inner_ref[...] = final[0]
    grad_outer_ref[...] = final[1]
    copies.finish()


def exchange(lifted, cot_coarse, inner, outer):
    eye = jnp.eye(256, dtype=jnp.bfloat16)
    vmem = pl.BlockSpec(memory_space=pltpu.VMEM)
    wide = (8, 2, CELLS, 1024)
    bf16, f32 = jnp.bfloat16, jnp.float32
    update, grad_inner, grad_outer = pl.pallas_call(
        exchange_kernel,
        out_shape=(
            jax.ShapeDtypeStruct((CELLS, 1024), bf16),
            jax.ShapeDtypeStruct((HALF, 256), f32),
            jax.ShapeDtypeStruct((HALF, 256), f32),
        ),
        in_specs=[vmem] * 5,
        out_specs=(vmem,) * 3,
        scratch_shapes=[
            pltpu.VMEM(wide, bf16),
            pltpu.VMEM(wide, bf16),
            pltpu.VMEM(wide, bf16),
            pltpu.VMEM((8, CELLS, 1024), bf16),
            pltpu.VMEM((2, 2, HALF, 1024), bf16),
            pltpu.VMEM((2, 2, CELLS, 1024), bf16),
            pltpu.VMEM((CELLS, 1024), bf16),
            pltpu.VMEM((256, 16 * CELLS), bf16),
            pltpu.VMEM((256, 16 * CELLS), bf16),
            pltpu.VMEM((8, 2, 256, 128), bf16),
            pltpu.VMEM((2, 256, 128), bf16),
            pltpu.VMEM((3, 2, 2, 256, 128), bf16),
            pltpu.VMEM((2, 2, HALF, 256), f32),
            pltpu.VMEM((2, 2, HALF, 256), bf16),
            pltpu.SemaphoreType.DMA((66,)),
            pltpu.SemaphoreType.DMA((66,)),
        ],
        compiler_params=pltpu.CompilerParams(
            collective_id=0, has_side_effects=True, vmem_limit_bytes=48 * 1024 * 1024
        ),
        name="exchange",
    )(lifted, cot_coarse, inner, outer, eye)
    return update, grad_inner, grad_outer.T


def local(
    features,
    land_mask,
    land_embed,
    window_shift,
    fine_gain,
    qkv_weight,
    bias_table,
    mix_weight,
    merge_gain,
    merge_weight,
    coarse_gain,
    inner_weight,
    outer_weight,
    expand_weight,
    cotangent,
):
    tile_rows, tile_cols, feat_width = features.shape
    offset = window_shift[0]
    position_bias = bias_matrix(bias_table, WH, WL)
    base_rows = features.astype(jnp.float32) + land_mask.astype(jnp.float32)[..., None] * land_embed
    normed = layer_norm(base_rows, fine_gain).astype(jnp.bfloat16)
    widened = with_halo(normed, (("lon", 1),), WL)
    chosen = lax.dynamic_slice_in_dim(widened, offset, tile_cols + WL, 1)
    attended_wide = window_attention(chosen, qkv_weight, position_bias, WH, WL, HEADS1)
    attended = lax.dynamic_slice_in_dim(attended_wide, WL - offset, tile_cols, 1)
    level_one = (
        base_rows + jnp.dot(attended, mix_weight, preferred_element_type=jnp.float32)
    ).astype(jnp.bfloat16)
    merged = layer_norm(fold_quads(level_one).astype(jnp.float32), merge_gain).astype(jnp.bfloat16)
    coarse_cells = jnp.dot(
        merged.reshape(-1, 4 * feat_width), merge_weight, preferred_element_type=jnp.float32
    ).astype(jnp.bfloat16)
    lifted = layer_norm(coarse_cells.astype(jnp.float32), coarse_gain).astype(jnp.bfloat16)
    cot_folded = fold_quads(cotangent).reshape(-1, 4 * feat_width)
    cot_coarse = lax.dot_general(
        cot_folded, expand_weight, (((1,), (1,)), ((), ())), preferred_element_type=jnp.float32
    ).astype(jnp.bfloat16)
    update, grad_inner, grad_outer = exchange(lifted, cot_coarse, inner_weight, outer_weight)
    update = update.astype(jnp.float32)
    back_cells = (coarse_cells.astype(jnp.float32) + update).astype(jnp.bfloat16)
    raised = jnp.dot(back_cells, expand_weight, preferred_element_type=jnp.float32).reshape(
        tile_rows // 2, tile_cols // 2, 4 * feat_width
    )
    prediction = (level_one.astype(jnp.float32) + unfold_quads(raised, feat_width)).astype(
        jnp.bfloat16
    )
    return (prediction, grad_inner, grad_outer)


def solution(mesh):
    return jax.shard_map(
        local,
        mesh=mesh,
        in_specs=(
            P("lat", "lon", None),
            P("lat", "lon"),
            P(),
            P(),
            P(),
            P(),
            P(),
            P(),
            P(),
            P(),
            P(),
            P(None, "lon"),
            P("lon", None),
            P(),
            P("lat", "lon", None),
        ),
        out_specs=(P("lat", "lon", None), P("lat", "lon"), P("lon", "lat")),
        check_vma=False,
    )
```

```python
import jax
import jax.numpy as jnp
from jax import lax
from jax.experimental import pallas as pl
from jax.experimental.pallas import tpu as pltpu
from jax.sharding import PartitionSpec as P

HEADS1 = 8
WH = 8
WL = 16
D1 = 512
D2 = 1024
ROWS = 16
COLS = 32
CELLS = 128
HALF = 64
QUART = 32
COPIES = 84

NORM_EPS = 1e-05
GELU_SCALE = 0.7978845608028654
MESH = pl.DeviceIdType.MESH
BF16 = jnp.bfloat16
F32 = jnp.float32
LAST = (((1,), (1,)), ((), ()))


def normalise(values):
    centre = jnp.mean(values, axis=-1, keepdims=True)
    centred = values - centre
    spread = jnp.mean(centred * centred, axis=-1, keepdims=True)
    return centred * lax.rsqrt(spread + NORM_EPS)


def gelu_pair(pre_act):
    square = pre_act * pre_act
    inner = GELU_SCALE * (pre_act + 0.044715 * square * pre_act)
    tangent = jnp.tanh(inner)
    half = 0.5 * (1.0 + tangent)
    value = pre_act * half
    slope = half + value * (1.0 - tangent) * (GELU_SCALE + (3.0 * 0.044715 * GELU_SCALE) * square)
    return (value, slope)


def matmul(a, b):
    return jnp.dot(a, b, preferred_element_type=F32)


def matmul_t(a, b):
    return lax.dot_general(a, b, LAST, preferred_element_type=F32)


class Copies:
    def __init__(self, send_sems, recv_sems):
        self.send_sems, self.recv_sems = send_sems, recv_sems
        self.places, self.started = {}, []

    def describe(self, name, src, dst, device):
        place = self.places.setdefault(name, len(self.places))
        return pltpu.make_async_remote_copy(
            src_ref=src,
            dst_ref=dst,
            send_sem=self.send_sems.at[place],
            recv_sem=self.recv_sems.at[place],
            device_id=device,
            device_id_type=MESH,
        )

    def start(self, name, src, dst, device):
        copy = self.describe(name, src, dst, device)
        copy.start()
        self.started.append(copy)

    def arrived(self, name, dst, device):
        self.describe(name, dst, dst, device).wait_recv()

    def finish(self):
        for copy in self.started:
            copy.wait_send()


def window_kernel(
    shift_ref, features_ref, mask_ref, embed_ref, fine_gain_ref, bias_rows_ref, merge_gain_ref,
    coarse_gain_ref, cotangent_ref, eye_ref,
    qkv_hbm, mix_hbm, merge_hbm, inner_hbm, outer_hbm, expand_hbm,
    prediction_ref, grad_inner_ref, grad_outer_ref,
    qkv_ref, mix_ref, merge_ref, inner_ref, outer_ref, expand_ref,
    base, normed, halo, wide, bias, window, projected, attended, shifted, level, merged, coarse, back,
    lift, cots, part, core_in, across_in, half_in, full_in, pair_in,
    hidden_t, cot_pre_t, terms, ring_half, ring_full, side_out, side_in,
    load_sems, send_sems, recv_sems,
):
    lon, lat = lax.axis_index("lon"), lax.axis_index("lat")
    core, y_hi, x = lon % 2, (lon // 2) % 2, lon // 4
    z, y_lo = lat // 2, lat % 2
    east, west = {"lon": (lon + 1) % 16}, {"lon": (lon + 15) % 16}
    partner = {"lon": lon + 1 - 2 * core}
    across = {"lon": lon + 2 - 4 * y_hi}
    right, left = {"lon": (lon + 4) % 16}, {"lon": (lon + 12) % 16}
    up, down = {"lat": (lat + 2) % 16}, {"lat": (lat + 14) % 16}
    side = {"lat": lat + 1 - 2 * y_lo}

    loads = {}
    for k, (name, src, dst) in enumerate(
        (
            ("expand", expand_hbm, expand_ref),
            ("qkv", qkv_hbm, qkv_ref),
            ("mix", mix_hbm, mix_ref),
            ("merge", merge_hbm, merge_ref),
            ("inner", inner_hbm, inner_ref),
            ("outer", outer_hbm, outer_ref),
        )
    ):
        loads[name] = pltpu.make_async_copy(src, dst, load_sems.at[k])
        loads[name].start()

    barrier = pltpu.get_barrier_semaphore()
    neighbours = (east, west, partner, across, right, left, up, down, side)
    for device in neighbours:
        pl.semaphore_signal(barrier, inc=1, device_id=device, device_id_type=MESH)

    diagonal = lax.broadcasted_iota(jnp.int32, (COLS, COLS), 0) == lax.broadcasted_iota(
        jnp.int32, (COLS, COLS), 1
    )

    @pl.loop(0, ROWS, unroll=2)
    def _(r):
        land = mask_ref[pl.ds(r, 1), :].astype(F32)
        land = jnp.sum(jnp.where(diagonal, land, 0.0), axis=1, keepdims=True)
        cells = features_ref[r].astype(F32) + land * embed_ref[...]
        base[r] = cells
        rounded = (normalise(cells) * fine_gain_ref[...]).astype(BF16)
        normed[r] = rounded
        wide[r, WL : WL + COLS, :] = rounded.astype(F32)

    pl.semaphore_wait(barrier, len(neighbours))
    copies = Copies(send_sems, recv_sems)
    copies.start("halo e", normed.at[:, pl.ds(COLS - WL, WL), :], halo.at[0], east)
    copies.start("halo w", normed.at[:, pl.ds(0, WL), :], halo.at[1], west)

    def chip(dx, dy):
        return ((x + dx) % 4) * 2 + (y_hi + dy) % 2

    def fold(store):
        @pl.loop(0, ROWS // 2)
        def _(r):
            store(
                r,
                [
                    jnp.concatenate(
                        [level[r, i, c, pl.ds(j, COLS // 2, stride=2), :] for c in range(4)], axis=1
                    )
                    for i in range(2)
                    for j in range(2)
                ],
            )

    @pl.loop(0, ROWS // 2)
    def _(r):
        for i in range(2):
            cells = cotangent_ref[2 * r + i].astype(F32)
            for c in range(4):
                level[r, i, c] = cells[:, c * 128 : (c + 1) * 128]

    def store_cot(r, quads):
        rows = pl.ds(pl.multiple_of(r * 16, 16), 16)
        for q in range(4):
            merged[rows, q * D1 : (q + 1) * D1] = quads[q].astype(BF16)

    fold(store_cot)
    loads["expand"].wait()

    @pl.loop(0, 4)
    def _(j):
        lanes = pl.ds(pl.multiple_of(j * 256, 256), 256)
        cots[chip(0, 0), core, :, lanes] = matmul_t(merged[...], expand_ref[lanes, :]).astype(BF16)

    low, high = pl.ds(0, HALF), pl.ds(HALF, HALF)
    first, second = pl.ds(0, QUART), pl.ds(QUART, QUART)

    class Gather:
        def __init__(self, name, array):
            self.name, self.array = name, array

        def at(self, dx, dy, rows=None, dk=0):
            block = self.array.at[chip(dx, dy), (core + dk) % 2]
            return block if rows is None else block.at[rows]

        def send(self, name, dx, dy, rows, device):
            block = self.at(dx, dy, rows)
            copies.start(self.name + name, block, block, device)

        def came(self, name, dx, dy, rows, device):
            copies.arrived(self.name + name, self.at(dx, dy, rows), device)

        def share(self, dx, dy):
            self.send("p%d%d" % (dx, dy), dx, dy, None, partner)

        def begin(self):
            self.send("yl", 0, 0, low, across)
            self.send("xr", 0, 0, None, right)
            self.send("xl", 0, 0, None, left)
            self.send("y0", 0, 0, high, across)
            self.share(0, 0)

        def near(self):
            self.came("xr", 3, 0, None, right)
            self.send("fr", 3, 0, low, right)
            self.send("y3", 3, 0, high, across)
            self.came("xl", 1, 0, None, left)
            self.send("fl", 1, 0, high, left)
            self.send("y1", 1, 0, high, across)
            self.share(3, 0)
            self.share(1, 0)

        def other(self):
            self.came("yl", 0, 1, low, across)
            self.send("or", 0, 1, low, right)
            self.send("ol", 0, 1, low, left)

        def far(self):
            self.came("fl", 2, 0, high, left)
            self.send("y2", 2, 0, high, across)
            self.came("fr", 2, 0, low, right)
            self.share(2, 0)

        def other_near(self):
            self.came("or", 3, 1, low, right)
            self.send("gr", 3, 1, first, right)
            self.came("ol", 1, 1, low, left)
            self.send("gl", 1, 1, second, left)
            self.came("y0", 0, 1, high, across)
            self.share(0, 1)
            self.came("y3", 3, 1, high, across)
            self.share(3, 1)
            self.came("y1", 1, 1, high, across)
            self.share(1, 1)

        def other_far(self):
            self.came("gr", 2, 1, first, right)
            self.came("gl", 2, 1, second, left)
            self.came("y2", 2, 1, high, across)
            self.share(2, 1)

        def shared(self, dx, dy):
            copies.arrived(self.name + "p%d%d" % (dx, dy), self.at(dx, dy, None, 1), partner)

    gather_cot, gather_lift = Gather("c", cots), Gather("l", lift)
    gather_cot.begin()

    lane = lax.broadcasted_iota(jnp.int32, (WL, 128), 1)

    @pl.loop(0, HEADS1)
    def _(h):
        halves = []
        for k in range(2):
            total = jnp.zeros((WL, 128), F32)
            for i in range(8 if k == 0 else 7):
                row = jnp.broadcast_to(bias_rows_ref[h, 8 * k + i : 8 * k + i + 1, :], (WL, 128))
                turned = pltpu.roll(row, (128 - 15 + 16 * i) % 128, 1, stride=1, stride_axis=0)
                total = jnp.where(lane // 16 == i, turned, total)
            halves.append(total)
        both = jnp.concatenate(halves, axis=1)
        for i in range(WH):
            start = (WH - 1 - i) * WL
            bias[h, i * WL : (i + 1) * WL, :] = both[:, start : start + 128]

    offset = shift_ref[0]
    first_head = lax.broadcasted_iota(jnp.int32, (CELLS, 128), 1) < 64
    ones = jnp.ones((CELLS, 128), BF16)

    def attend(w):
        @pl.loop(0, ROWS, unroll=2)
        def _(r):
            cells = wide[r, w * WL : (w + 2) * WL, :]
            window[r] = pltpu.roll(cells, 2 * WL - offset, 0)[:WL].astype(BF16)

        @pl.loop(0, 6)
        def _(j):
            lanes = pl.ds(pl.multiple_of(j * 256, 256), 256)
            rows = window[...].reshape(ROWS * WL, D1)
            projected[:, lanes] = matmul(rows, qkv_ref[:, lanes]).astype(BF16)

        @pl.loop(0, 8, unroll=2)
        def _(k):
            band, pair = k // 4, k % 4
            rows = pl.ds(pl.multiple_of(band * CELLS, CELLS), CELLS)

            def lanes(kind):
                return pl.ds(pl.multiple_of(kind * D1 + pair * 128, 128), 128)

            queries = projected[rows, lanes(0)]
            zero = jnp.zeros_like(queries)
            queries = jnp.concatenate(
                [jnp.where(first_head, queries, zero), jnp.where(first_head, zero, queries)], axis=0
            )
            scores = matmul_t(queries, projected[rows, lanes(1)]) * 0.125
            scores = scores + bias[pl.ds(2 * pair, 2)].reshape(2 * CELLS, 128)
            expo = jnp.exp(scores - jnp.max(scores, axis=1, keepdims=True)).astype(BF16)
            values = jnp.concatenate([projected[rows, lanes(2)], ones], axis=1)
            sums = matmul(expo, values)
            heads = sums[:, :128] / sums[:, 128:]
            heads = jnp.where(first_head, heads[:CELLS], heads[CELLS:])
            attended[pl.ds(band * WH, WH), w * WL : (w + 1) * WL, lanes(0)] = heads.reshape(
                WH, WL, 128
            )

    loads["qkv"].wait()
    attend(1)
    gather_cot.near()
    copies.arrived("halo e", halo.at[0], east)
    copies.arrived("halo w", halo.at[1], west)

    @pl.loop(0, ROWS)
    def _(r):
        wide[r, 0:WL, :] = halo[0, r].astype(F32)
        wide[r, WL + COLS :, :] = halo[1, r].astype(F32)

    attend(0)
    gather_cot.other()
    attend(2)
    gather_cot.far()

    loads["mix"].wait()

    @pl.loop(0, ROWS, unroll=2)
    def _(r):
        shifted[r] = pltpu.roll(attended[r], COLS + offset, 0)[:COLS].astype(BF16)

    @pl.loop(0, 4)
    def _(i):
        rows = pl.ds(i * 4, 4)
        mixed = matmul(shifted[rows].reshape(CELLS, D1), mix_ref[...]).reshape(4, COLS, D1)
        mixed = (base[rows] + mixed).astype(BF16).astype(F32).reshape(2, 2, COLS, D1)
        for c in range(4):
            level[pl.ds(i * 2, 2), :, c] = mixed[..., c * 128 : (c + 1) * 128]

    def store_merged(r, quads):
        centre = sum(jnp.sum(quad, axis=1, keepdims=True) for quad in quads) / (4 * D1)
        quads = [quad - centre for quad in quads]
        spread = sum(jnp.sum(quad * quad, axis=1, keepdims=True) for quad in quads) / (4 * D1)
        scale = lax.rsqrt(spread + NORM_EPS)
        rows = pl.ds(pl.multiple_of(r * 16, 16), 16)
        for q in range(4):
            lanes = slice(q * D1, (q + 1) * D1)
            merged[rows, lanes] = (quads[q] * scale * merge_gain_ref[:, lanes]).astype(BF16)

    fold(store_merged)
    loads["merge"].wait()

    @pl.loop(0, 4)
    def _(j):
        lanes = pl.ds(pl.multiple_of(j * 256, 256), 256)
        coarse[:, lanes] = matmul(merged[...], merge_ref[:, lanes]).astype(BF16)

    @pl.loop(0, 4)
    def _(i):
        rows = pl.ds(pl.multiple_of(i * 32, 32), 32)
        lift[chip(0, 0), core, rows, :] = (
            normalise(coarse[rows, :].astype(F32)) * coarse_gain_ref[...]
        ).astype(BF16)

    gather_lift.begin()
    gather_cot.other_near()
    loads["inner"].wait()
    loads["outer"].wait()

    def process(dx, dy):
        gather_cot.shared(dx, dy)
        gather_lift.shared(dx, dy)
        p = chip(dx, dy)
        pre = matmul(lift[p].reshape(2 * CELLS, D2), inner_ref[...])
        value, slope = gelu_pair(pre)
        hidden = value.astype(BF16)
        part[p] = matmul(hidden, outer_ref[...]).astype(BF16).reshape(2, CELLS, D2)
        copies.start("s%d%d" % (dx, dy), part.at[p, 1 - core], core_in.at[p], partner)
        cot_hidden = matmul_t(cots[p].reshape(2 * CELLS, D2), outer_ref[...])
        cot_pre = (cot_hidden * slope).astype(BF16)
        columns = pl.ds(pl.multiple_of(p * 2 * CELLS, 2 * CELLS), 2 * CELLS)
        hidden_t[:, columns] = matmul_t(eye_ref[...], hidden).astype(BF16)
        cot_pre_t[:, columns] = matmul_t(eye_ref[...], cot_pre).astype(BF16)

    process(0, 0)
    gather_lift.near()
    gather_cot.other_far()
    gather_lift.other()
    process(3, 0)
    process(1, 0)
    gather_lift.far()
    process(2, 0)
    gather_lift.other_near()
    process(0, 1)
    process(3, 1)
    process(1, 1)
    gather_lift.other_far()
    process(2, 1)

    def add_to(place, rows, *others):
        total = part[place, core, rows, :].astype(F32)
        for other in others:
            total = total + other.astype(F32)
        part[place, core, rows, :] = total.astype(BF16)

    def cores(dx, dy):
        p = chip(dx, dy)
        copies.arrived("s%d%d" % (dx, dy), core_in.at[p], partner)
        add_to(p, slice(None), core_in[p])
        if dy == 1:
            block = part.at[p, core, high]
            copies.start("t%d" % dx, block, across_in.at[dx], across)

    def from_across(dx):
        copies.arrived("t%d" % dx, across_in.at[dx], across)
        add_to(chip(dx, 0), high, across_in[dx])

    class Chain:
        def __init__(self, name, place, dy, start):
            self.name, self.place, self.dy = name, place, dy
            self.rows = pl.ds(start, HALF)
            self.firsts, self.seconds = pl.ds(start, QUART), pl.ds(start + QUART, QUART)

        def begin(self):
            block = part.at[chip(2, self.dy), core]
            here = half_in.at[self.place]
            copies.start(self.name + "0", block.at[self.firsts], here.at[0], right)
            copies.start(self.name + "1", block.at[self.seconds], here.at[1], left)

        def next(self):
            here, there = half_in.at[self.place], full_in.at[self.place]
            for way, device, dx, rows in (
                (0, right, 1, self.firsts),
                (1, left, 3, self.seconds),
            ):
                copies.arrived(self.name + "%d" % way, here.at[way], device)
                p = chip(dx, self.dy)
                add_to(p, rows, here[way])
                copies.start(
                    self.name + "%d" % (2 + way),
                    part.at[p, core, self.rows],
                    there.at[way],
                    device,
                )

        def end(self):
            there = full_in.at[self.place]
            copies.arrived(self.name + "2", there.at[0], right)
            copies.arrived(self.name + "3", there.at[1], left)
            return (
                part[chip(0, self.dy), core, self.rows, :].astype(F32)
                + there[0].astype(F32)
                + there[1].astype(F32)
            )

    away, here_low, here_high = Chain("a", 0, 1, 0), Chain("b", 1, 0, 0), Chain("d", 2, 0, HALF)

    def zed(dz):
        return (z + dz) % 8

    def ring(step):
        if step == 0:
            distant = terms.at[zed(4)]
            copies.start("z00", distant.at[0], ring_half.at[0], up)
            copies.start("z01", distant.at[1], ring_half.at[1], down)
            return
        for way, device, mine in ((0, up, zed(4 - step)), (1, down, zed(4 + step))):
            name = "z%d%d" % (step - 1, way)
            if step == 1:
                copies.arrived(name, ring_half.at[way], device)
                terms[mine, way] = (
                    terms[mine, way].astype(F32) + ring_half[way].astype(F32)
                ).astype(BF16)
            else:
                copies.arrived(name, ring_full.at[step - 2, way], device)
                terms[mine] = (
                    terms[mine].astype(F32) + ring_full[step - 2, way].astype(F32)
                ).astype(BF16)
            copies.start("z%d%d" % (step, way), terms.at[mine], ring_full.at[step - 1, way], device)

    def ring_end():
        total = terms[z].astype(F32)
        for way, device in ((0, up), (1, down)):
            copies.arrived("z3%d" % way, ring_full.at[2, way], device)
            total = total + ring_full[2, way].astype(F32)
        for kind in range(2):
            side_out[kind] = total[kind].T.reshape(2, HALF, 256)
        side_in[1] = side_out[:, 1 - y_lo].astype(BF16)
        copies.start("side", side_in.at[1], side_in.at[0], side)

    cores(2, 1)
    away.begin()
    cores(1, 1)
    cores(3, 1)
    cores(0, 1)
    cores(2, 0)
    here_low.begin()

    @pl.loop(0, 4)
    def _(j):
        lanes = pl.ds(pl.multiple_of(j * 256, 256), 256)
        for kind, rows, array in ((0, cot_pre_t, lift), (1, hidden_t, cots)):
            term = matmul(rows[...], array[:, :, :, lanes].reshape(16 * CELLS, 256)).astype(BF16)
            terms[2 * j, kind] = term[:, :128]
            terms[2 * j + 1, kind] = term[:, 128:]

    ring(0)
    away.next()
    cores(1, 0)
    cores(3, 0)
    here_low.next()
    from_across(2)
    here_high.begin()
    ring(1)
    part[chip(0, 1), core, low, :] = away.end().astype(BF16)
    copies.start("pair", part.at[chip(0, 1), core, low], pair_in, across)
    ring(2)
    from_across(1)
    from_across(3)
    here_high.next()
    cores(0, 0)
    ring(3)
    loads_done = here_low.end()
    from_across(0)
    copies.arrived("pair", pair_in, across)
    back[low, :] = (
        coarse[low, :].astype(F32) + loads_done + pair_in[...].astype(F32)
    ).astype(BF16)
    ring_end()
    back[high, :] = (coarse[high, :].astype(F32) + here_high.end()).astype(BF16)

    for q in range(4):
        raised = matmul(back[...], expand_ref[:, q * D1 : (q + 1) * D1])
        cells = pl.ds(q % 2, COLS // 2, stride=2)
        for c in range(4):
            block = raised[:, c * 128 : (c + 1) * 128].reshape(ROWS // 2, COLS // 2, 128)
            level[:, q // 2, c, cells, :] = level[:, q // 2, c, cells, :] + block

    @pl.loop(0, ROWS // 2)
    def _(r):
        for i in range(2):
            for c in range(4):
                prediction_ref[2 * r + i, :, c * 128 : (c + 1) * 128] = level[r, i, c].astype(BF16)

    copies.arrived("side", side_in.at[0], side)
    final = side_out[:, y_lo] + side_in[0].astype(F32)
    grad_inner_ref[...] = final[0]
    grad_outer_ref[...] = final[1].T
    copies.finish()


def local(
    features, land_mask, land_embed, window_shift, fine_gain, qkv_weight, bias_table, mix_weight,
    merge_gain, merge_weight, coarse_gain, inner_weight, outer_weight, expand_weight, cotangent,
):
    vmem = pl.BlockSpec(memory_space=pltpu.VMEM)
    smem = pl.BlockSpec(memory_space=pltpu.SMEM)
    anywhere = pl.BlockSpec(memory_space=pl.ANY)
    reach = 2 * WL - 1
    bias_rows = jnp.pad(
        bias_table[:, ::-1].reshape(HEADS1, 2 * WH - 1, reach), ((0, 0), (0, 1), (0, 128 - reach))
    )
    wide_block = pltpu.VMEM((8, 2, CELLS, D2), BF16)
    return pl.pallas_call(
        window_kernel,
        out_shape=(
            jax.ShapeDtypeStruct((ROWS, COLS, D1), BF16),
            jax.ShapeDtypeStruct((HALF, 256), F32),
            jax.ShapeDtypeStruct((256, HALF), F32),
        ),
        in_specs=[smem] + [vmem] * 9 + [anywhere] * 6,
        out_specs=(vmem,) * 3,
        scratch_shapes=[
            pltpu.VMEM((D1, 3 * D1), BF16),
            pltpu.VMEM((D1, D1), BF16),
            pltpu.VMEM((4 * D1, D2), BF16),
            pltpu.VMEM((D2, 256), BF16),
            pltpu.VMEM((256, D2), BF16),
            pltpu.VMEM((D2, 4 * D1), BF16),
            pltpu.VMEM((ROWS, COLS, D1), F32),
            pltpu.VMEM((ROWS, COLS, D1), BF16),
            pltpu.VMEM((2, ROWS, WL, D1), BF16),
            pltpu.VMEM((ROWS, COLS + 2 * WL, D1), F32),
            pltpu.VMEM((HEADS1, CELLS, CELLS), F32),
            pltpu.VMEM((ROWS, WL, D1), BF16),
            pltpu.VMEM((ROWS * WL, 3 * D1), BF16),
            pltpu.VMEM((ROWS, COLS + WL, D1), F32),
            pltpu.VMEM((ROWS, COLS, D1), BF16),
            pltpu.VMEM((ROWS // 2, 2, 4, COLS, 128), F32),
            pltpu.VMEM((CELLS, 4 * D1), BF16),
            pltpu.VMEM((CELLS, D2), BF16),
            pltpu.VMEM((CELLS, D2), BF16),
            wide_block,
            wide_block,
            wide_block,
            pltpu.VMEM((8, CELLS, D2), BF16),
            pltpu.VMEM((4, HALF, D2), BF16),
            pltpu.VMEM((3, 2, QUART, D2), BF16),
            pltpu.VMEM((3, 2, HALF, D2), BF16),
            pltpu.VMEM((HALF, D2), BF16),
            pltpu.VMEM((256, 16 * CELLS), BF16),
            pltpu.VMEM((256, 16 * CELLS), BF16),
            pltpu.VMEM((8, 2, 256, 128), BF16),
            pltpu.VMEM((2, 256, 128), BF16),
            pltpu.VMEM((3, 2, 2, 256, 128), BF16),
            pltpu.VMEM((2, 2, HALF, 256), F32),
            pltpu.VMEM((2, 2, HALF, 256), BF16),
            pltpu.SemaphoreType.DMA((6,)),
            pltpu.SemaphoreType.DMA((COPIES,)),
            pltpu.SemaphoreType.DMA((COPIES,)),
        ],
        compiler_params=pltpu.CompilerParams(
            collective_id=0, has_side_effects=True, vmem_limit_bytes=56 * 1024 * 1024
        ),
        name="window",
    )(
        window_shift, features, land_mask, land_embed[None], fine_gain[None], bias_rows,
        merge_gain[None], coarse_gain[None], cotangent, jnp.eye(256, dtype=BF16),
        qkv_weight, mix_weight, merge_weight, inner_weight, outer_weight, expand_weight,
    )


def solution(mesh):
    return jax.shard_map(
        local,
        mesh=mesh,
        in_specs=(
            P("lat", "lon", None),
            P("lat", "lon"),
            P(),
            P(),
            P(),
            P(),
            P(),
            P(),
            P(),
            P(),
            P(),
            P(None, "lon"),
            P("lon", None),
            P(),
            P("lat", "lon", None),
        ),
        out_specs=(P("lat", "lon", None), P("lat", "lon"), P("lon", "lat")),
        check_vma=False,
    )
```

```python
import jax
import jax.numpy as jnp
from jax import lax
from jax.experimental import pallas as pl
from jax.experimental.pallas import tpu as pltpu
from jax.sharding import PartitionSpec as P

HEADS1 = 8
WH = 8
WL = 16
D1 = 512
D2 = 1024
ROWS = 16
COLS = 32
CELLS = 128
HALF = 64
QUART = 32
COPIES = 96

NORM_EPS = 1e-05
GELU_SCALE = 0.7978845608028654
MESH = pl.DeviceIdType.MESH
BF16 = jnp.bfloat16
F32 = jnp.float32
LAST = (((1,), (1,)), ((), ()))


def normalise(values):
    centre = jnp.mean(values, axis=-1, keepdims=True)
    centred = values - centre
    spread = jnp.mean(centred * centred, axis=-1, keepdims=True)
    return centred * lax.rsqrt(spread + NORM_EPS)


def gelu_pair(pre_act):
    square = pre_act * pre_act
    inner = GELU_SCALE * (pre_act + 0.044715 * square * pre_act)
    tangent = jnp.tanh(inner)
    half = 0.5 * (1.0 + tangent)
    value = pre_act * half
    slope = half + value * (1.0 - tangent) * (GELU_SCALE + (3.0 * 0.044715 * GELU_SCALE) * square)
    return (value, slope)


def matmul(a, b):
    return jnp.dot(a, b, preferred_element_type=F32)


def matmul_t(a, b):
    return lax.dot_general(a, b, LAST, preferred_element_type=F32)


class Copies:
    def __init__(self, send_sems, recv_sems):
        self.send_sems, self.recv_sems = send_sems, recv_sems
        self.places, self.started = {}, []

    def describe(self, name, src, dst, device):
        place = self.places.setdefault(name, len(self.places))
        return pltpu.make_async_remote_copy(
            src_ref=src,
            dst_ref=dst,
            send_sem=self.send_sems.at[place],
            recv_sem=self.recv_sems.at[place],
            device_id=device,
            device_id_type=MESH,
        )

    def start(self, name, src, dst, device):
        copy = self.describe(name, src, dst, device)
        copy.start()
        self.started.append(copy)

    def arrived(self, name, dst, device):
        self.describe(name, dst, dst, device).wait_recv()

    def finish(self):
        for copy in self.started:
            copy.wait_send()


def window_kernel(
    shift_ref, features_ref, mask_ref, embed_ref, fine_gain_ref, table_ref, merge_gain_ref,
    coarse_gain_ref, cotangent_ref,
    qkv_hbm, mix_hbm, merge_hbm, inner_hbm, outer_hbm, expand_hbm,
    prediction_ref, grad_inner_ref, grad_outer_ref,
    qkv_ref, mix_ref, merge_ref, inner_ref, outer_ref, expand_ref,
    padded, table_rows, base, normed, halo, wide, bias, window, projected, attended, shifted, level, merged, coarse, back,
    lift, cots, part, core_in, across_in, half_in, full_in, pair_in,
    hidden_t, cot_pre_t, sums, terms, ring_in, side_out, side_in,
    load_sems, send_sems, recv_sems,
):
    lon, lat = lax.axis_index("lon"), lax.axis_index("lat")
    core, y_hi, x = lon % 2, (lon // 2) % 2, lon // 4
    z, y_lo = lat // 2, lat % 2
    east, west = {"lon": (lon + 1) % 16}, {"lon": (lon + 15) % 16}
    partner = {"lon": lon + 1 - 2 * core}
    across = {"lon": lon + 2 - 4 * y_hi}
    right, left = {"lon": (lon + 4) % 16}, {"lon": (lon + 12) % 16}
    up, down = {"lat": (lat + 2) % 16}, {"lat": (lat + 14) % 16}
    side = {"lat": lat + 1 - 2 * y_lo}

    loads = {}
    for k, (name, src, dst) in enumerate(
        (
            ("expand", expand_hbm, expand_ref),
            ("qkv", qkv_hbm, qkv_ref),
            ("mix", mix_hbm, mix_ref),
            ("merge", merge_hbm, merge_ref),
            ("inner", inner_hbm, inner_ref),
            ("outer", outer_hbm, outer_ref),
        )
    ):
        loads[name] = pltpu.make_async_copy(src, dst, load_sems.at[k])
        loads[name].start()

    barrier = pltpu.get_barrier_semaphore()
    neighbours = (east, west, partner, across, right, left, up, down, side)
    for device in neighbours:
        pl.semaphore_signal(barrier, inc=1, device_id=device, device_id_type=MESH)

    diagonal = lax.broadcasted_iota(jnp.int32, (COLS, COLS), 0) == lax.broadcasted_iota(
        jnp.int32, (COLS, COLS), 1
    )

    @pl.loop(0, ROWS, unroll=2)
    def _(r):
        land = mask_ref[pl.ds(r, 1), :].astype(F32)
        land = jnp.sum(jnp.where(diagonal, land, 0.0), axis=1, keepdims=True)
        cells = features_ref[r].astype(F32) + land * embed_ref[...]
        base[r] = cells
        rounded = (normalise(cells) * fine_gain_ref[...]).astype(BF16)
        normed[r] = rounded
        wide[r, WL : WL + COLS, :] = rounded.astype(F32)

    pl.semaphore_wait(barrier, len(neighbours))
    copies = Copies(send_sems, recv_sems)
    copies.start("halo e", normed.at[:, pl.ds(COLS - WL, WL), :], halo.at[0], east)
    copies.start("halo w", normed.at[:, pl.ds(0, WL), :], halo.at[1], west)

    padded[...] = jnp.zeros_like(padded)
    padded[:, 0 : table_ref.shape[1]] = table_ref[...]
    offsets = padded[...]
    top = offsets.astype(BF16)
    rest = offsets - top.astype(F32)
    middle = rest.astype(BF16)
    bottom = (rest - middle.astype(F32)).astype(BF16)
    turn = lax.broadcasted_iota(jnp.int32, (512, 640), 0) + lax.broadcasted_iota(
        jnp.int32, (512, 640), 1
    )
    turn = jnp.where(turn == table_ref.shape[1] - 1, 1.0, 0.0).astype(BF16)
    flipped = matmul(top, turn) + matmul(middle, turn) + matmul(bottom, turn)
    for i in range(2 * WH - 1):
        start = i * (2 * WL - 1)
        table_rows[i] = flipped[:, start : start + 128]
    lane = lax.broadcasted_iota(jnp.int32, (WL, 128), 1)

    @pl.loop(0, HEADS1)
    def _(h):
        halves = []
        for k in range(2):
            total = jnp.zeros((WL, 128), F32)
            for i in range(8 if k == 0 else 7):
                row = jnp.broadcast_to(table_rows[8 * k + i, pl.ds(h, 1), :], (WL, 128))
                turned = pltpu.roll(row, (128 - 15 + 16 * i) % 128, 1, stride=1, stride_axis=0)
                total = jnp.where(lane // 16 == i, turned, total)
            halves.append(total)
        both = jnp.concatenate(halves, axis=1)
        for i in range(WH):
            start = (WH - 1 - i) * WL
            bias[h, i * WL : (i + 1) * WL, :] = both[:, start : start + 128]

    def place(dx, dy):
        return 4 * dy + (0, 1, 3, 2)[dx % 4]

    def fold(store):
        @pl.loop(0, ROWS // 2)
        def _(r):
            store(
                r,
                [
                    jnp.concatenate(
                        [level[r, i, c, pl.ds(j, COLS // 2, stride=2), :] for c in range(4)], axis=1
                    )
                    for i in range(2)
                    for j in range(2)
                ],
            )

    @pl.loop(0, ROWS // 2)
    def _(r):
        for i in range(2):
            cells = cotangent_ref[2 * r + i].astype(F32)
            for c in range(4):
                level[r, i, c] = cells[:, c * 128 : (c + 1) * 128]

    def store_cot(r, quads):
        rows = pl.ds(pl.multiple_of(r * 16, 16), 16)
        for q in range(4):
            merged[rows, q * D1 : (q + 1) * D1] = quads[q].astype(BF16)

    fold(store_cot)
    loads["expand"].wait()

    @pl.loop(0, 4)
    def _(j):
        lanes = pl.ds(pl.multiple_of(j * 256, 256), 256)
        cots[0, 0, :, lanes] = matmul_t(merged[...], expand_ref[lanes, :]).astype(BF16)

    low, high = pl.ds(0, 80), pl.ds(80, 48)
    front, rear = pl.ds(0, HALF), pl.ds(HALF, HALF)
    ahead, behind = pl.ds(0, 48), pl.ds(48, 32)
    moves = {"r": (right, -1, 0, 0), "l": (left, 1, 0, 0), "y": (across, 0, 1, 0), "p": (partner, 0, 0, 1)}

    class Gather:
        def __init__(self, name, array):
            self.name, self.array = name, array

        def at(self, dx, dy, rows=None, dk=0):
            block = self.array.at[place(dx, dy), dk]
            return block if rows is None else block.at[rows]

        def send(self, name, dx, dy, rows, way):
            device, mx, my, mk = moves[way]
            there = self.at(dx + mx, (dy + my) % 2, rows, mk)
            copies.start(self.name + name, self.at(dx, dy, rows), there, device)

        def came(self, name, dx, dy, rows, way):
            copies.arrived(self.name + name, self.at(dx, dy, rows), moves[way][0])

        def share(self, dx, dy):
            self.send("p%d%d" % (dx, dy), dx, dy, None, "p")

        def shared(self, dx, dy):
            copies.arrived(self.name + "p%d%d" % (dx, dy), self.at(dx, dy, None, 1), partner)

        def begin(self):
            self.send("yl", 0, 0, low, "y")
            self.send("r0", 0, 0, front, "r")
            self.send("l0", 0, 0, rear, "l")
            self.send("r1", 0, 0, rear, "r")
            self.send("l1", 0, 0, front, "l")
            self.send("y0", 0, 0, high, "y")
            self.share(0, 0)

        def near(self):
            self.came("r0", 3, 0, front, "r")
            self.send("fr", 3, 0, front, "r")
            self.came("l0", 1, 0, rear, "l")
            self.send("fl", 1, 0, rear, "l")
            self.send("y1", 1, 0, high, "y")

        def other(self):
            self.came("yl", 0, 1, low, "y")
            self.send("or0", 0, 1, ahead, "r")
            self.send("ol0", 0, 1, behind, "l")
            self.send("or1", 0, 1, behind, "r")
            self.send("ol1", 0, 1, ahead, "l")

        def near_rest(self):
            self.came("r1", 3, 0, rear, "r")
            self.send("y3", 3, 0, high, "y")
            self.share(3, 0)
            self.came("l1", 1, 0, front, "l")
            self.share(1, 0)

        def far(self):
            self.came("fl", 2, 0, rear, "l")
            self.send("y2", 2, 0, high, "y")
            self.came("fr", 2, 0, front, "r")
            self.share(2, 0)

        def other_near(self):
            self.came("or0", 3, 1, ahead, "r")
            self.send("gr", 3, 1, ahead, "r")
            self.came("ol0", 1, 1, behind, "l")
            self.send("gl", 1, 1, behind, "l")
            self.came("y0", 0, 1, high, "y")
            self.share(0, 1)

        def other_rest(self):
            self.came("or1", 3, 1, behind, "r")
            self.came("ol1", 1, 1, ahead, "l")
            self.came("y1", 1, 1, high, "y")
            self.share(1, 1)
            self.came("y3", 3, 1, high, "y")
            self.share(3, 1)

        def other_far(self):
            self.came("y2", 2, 1, high, "y")
            self.came("gr", 2, 1, ahead, "r")
            self.came("gl", 2, 1, behind, "l")
            self.share(2, 1)

    gather_cot, gather_lift = Gather("c", cots), Gather("l", lift)
    gather_cot.begin()

    offset = shift_ref[0]
    first_head = lax.broadcasted_iota(jnp.int32, (CELLS, 128), 1) < 64
    ones = jnp.ones((CELLS, 128), BF16)

    def attend(w):
        @pl.loop(0, ROWS, unroll=2)
        def _(r):
            cells = wide[r, w * WL : (w + 2) * WL, :]
            window[r] = pltpu.roll(cells, 2 * WL - offset, 0)[:WL].astype(BF16)

        @pl.loop(0, 6)
        def _(j):
            lanes = pl.ds(pl.multiple_of(j * 256, 256), 256)
            rows = window[...].reshape(ROWS * WL, D1)
            projected[:, lanes] = matmul(rows, qkv_ref[:, lanes]).astype(BF16)

        @pl.loop(0, 8, unroll=4)
        def _(k):
            band, pair = k // 4, k % 4
            rows = pl.ds(pl.multiple_of(band * CELLS, CELLS), CELLS)

            def lanes(kind):
                return pl.ds(pl.multiple_of(kind * D1 + pair * 128, 128), 128)

            queries = projected[rows, lanes(0)] * 0.125
            zero = jnp.zeros_like(queries)
            queries = jnp.concatenate(
                [jnp.where(first_head, queries, zero), jnp.where(first_head, zero, queries)], axis=0
            )
            scores = matmul_t(queries, projected[rows, lanes(1)])
            scores = scores + bias[pl.ds(2 * pair, 2)].reshape(2 * CELLS, 128)
            expo = jnp.exp(scores - jnp.max(scores, axis=1, keepdims=True)).astype(BF16)
            values = jnp.concatenate([projected[rows, lanes(2)], ones], axis=1)
            sums = matmul(expo, values)
            heads = sums[:, :128] / sums[:, 128:]
            heads = jnp.where(first_head, heads[:CELLS], heads[CELLS:])
            attended[pl.ds(band * WH, WH), w * WL : (w + 1) * WL, lanes(0)] = heads.reshape(
                WH, WL, 128
            )

    loads["qkv"].wait()
    attend(1)
    gather_cot.near()
    gather_cot.other()
    copies.arrived("halo e", halo.at[0], east)
    copies.arrived("halo w", halo.at[1], west)

    @pl.loop(0, ROWS)
    def _(r):
        wide[r, 0:WL, :] = halo[0, r].astype(F32)
        wide[r, WL + COLS :, :] = halo[1, r].astype(F32)

    attend(0)
    gather_cot.near_rest()
    attend(2)
    gather_cot.far()
    gather_cot.other_near()

    loads["mix"].wait()

    @pl.loop(0, ROWS, unroll=2)
    def _(r):
        shifted[r] = pltpu.roll(attended[r], COLS + offset, 0)[:COLS].astype(BF16)

    @pl.loop(0, 4)
    def _(i):
        rows = pl.ds(i * 4, 4)
        mixed = matmul(shifted[rows].reshape(CELLS, D1), mix_ref[...]).reshape(4, COLS, D1)
        mixed = (base[rows] + mixed).astype(BF16).astype(F32).reshape(2, 2, COLS, D1)
        for c in range(4):
            level[pl.ds(i * 2, 2), :, c] = mixed[..., c * 128 : (c + 1) * 128]

    def store_merged(r, quads):
        centre = sum(jnp.sum(quad, axis=1, keepdims=True) for quad in quads) / (4 * D1)
        quads = [quad - centre for quad in quads]
        spread = sum(jnp.sum(quad * quad, axis=1, keepdims=True) for quad in quads) / (4 * D1)
        scale = lax.rsqrt(spread + NORM_EPS)
        rows = pl.ds(pl.multiple_of(r * 16, 16), 16)
        for q in range(4):
            lanes = slice(q * D1, (q + 1) * D1)
            merged[rows, lanes] = (quads[q] * scale * merge_gain_ref[:, lanes]).astype(BF16)

    fold(store_merged)
    loads["merge"].wait()

    @pl.loop(0, 4)
    def _(j):
        lanes = pl.ds(pl.multiple_of(j * 256, 256), 256)
        coarse[:, lanes] = matmul(merged[...], merge_ref[:, lanes]).astype(BF16)

    @pl.loop(0, 4)
    def _(i):
        rows = pl.ds(pl.multiple_of(i * 32, 32), 32)
        lift[0, 0, rows, :] = (
            normalise(coarse[rows, :].astype(F32)) * coarse_gain_ref[...]
        ).astype(BF16)

    gather_lift.begin()
    gather_cot.other_rest()
    loads["inner"].wait()
    loads["outer"].wait()

    unit = lax.broadcasted_iota(jnp.int32, (256, 256), 0) == lax.broadcasted_iota(
        jnp.int32, (256, 256), 1
    )
    unit = jnp.where(unit, 1.0, 0.0).astype(BF16)

    def process(dx, dy):
        gather_cot.shared(dx, dy)
        gather_lift.shared(dx, dy)
        p = place(dx, dy)
        pre = matmul(lift[p].reshape(2 * CELLS, D2), inner_ref[...])
        value, slope = gelu_pair(pre)
        hidden = value.astype(BF16)
        part[p] = matmul(hidden, outer_ref[...]).astype(BF16).reshape(2, CELLS, D2)
        copies.start("s%d%d" % (dx, dy), part.at[p, 1], core_in.at[p], partner)
        cot_hidden = matmul_t(cots[p].reshape(2 * CELLS, D2), outer_ref[...])
        cot_pre = (cot_hidden * slope).astype(BF16)
        columns = slice(p * 2 * CELLS, (p + 1) * 2 * CELLS)
        hidden_t[:, columns] = matmul_t(unit, hidden).astype(BF16)
        cot_pre_t[:, columns] = matmul_t(unit, cot_pre).astype(BF16)

    def gradients(begin, end):
        @pl.loop(0, 4)
        def _(j):
            lanes = pl.ds(pl.multiple_of(j * 256, 256), 256)
            for kind, rows, array in ((0, cot_pre_t, lift), (1, hidden_t, cots)):
                cells = array[begin:end, :, :, lanes].reshape((end - begin) * 2 * CELLS, 256)
                term = matmul(rows[:, begin * 2 * CELLS : end * 2 * CELLS], cells)
                if begin > 0:
                    term = term + sums[kind, :, lanes]
                if end < 8:
                    sums[kind, :, lanes] = term
                else:
                    terms[2 * j, kind] = term[:, :128].astype(BF16)
                    terms[2 * j + 1, kind] = term[:, 128:].astype(BF16)

    lower, upper = pl.ds(0, HALF), pl.ds(HALF, HALF)

    def add_to(p, rows, *others):
        total = part[p, 0, rows, :].astype(F32)
        for other in others:
            total = total + other.astype(F32)
        part[p, 0, rows, :] = total.astype(BF16)

    def cores(dx, dy):
        p = place(dx, dy)
        copies.arrived("s%d%d" % (dx, dy), core_in.at[p], partner)
        add_to(p, slice(None), core_in[p])
        if dy == 1:
            copies.start("t%d" % dx, part.at[p, 0, upper], across_in.at[dx], across)

    def from_across(dx):
        copies.arrived("t%d" % dx, across_in.at[dx], across)
        add_to(place(dx, 0), upper, across_in[dx])

    class Chain:
        def __init__(self, name, number, dy, start):
            self.name, self.number, self.dy = name, number, dy
            self.rows = pl.ds(start, HALF)
            self.firsts, self.seconds = pl.ds(start, QUART), pl.ds(start + QUART, QUART)

        def begin(self):
            block = part.at[place(2, self.dy), 0]
            here = half_in.at[self.number]
            copies.start(self.name + "0", block.at[self.firsts], here.at[0], right)
            copies.start(self.name + "1", block.at[self.seconds], here.at[1], left)

        def next(self):
            here, there = half_in.at[self.number], full_in.at[self.number]
            for way, device, dx, rows in (
                (0, right, 1, self.firsts),
                (1, left, 3, self.seconds),
            ):
                copies.arrived(self.name + "%d" % way, here.at[way], device)
                p = place(dx, self.dy)
                add_to(p, rows, here[way])
                copies.start(
                    self.name + "%d" % (2 + way),
                    part.at[p, 0, self.rows],
                    there.at[way],
                    device,
                )

        def end(self):
            there = full_in.at[self.number]
            copies.arrived(self.name + "2", there.at[0], right)
            copies.arrived(self.name + "3", there.at[1], left)
            return (
                part[place(0, self.dy), 0, self.rows, :].astype(F32)
                + there[0].astype(F32)
                + there[1].astype(F32)
            )

    away, here_low, here_high = Chain("a", 0, 1, 0), Chain("b", 1, 0, 0), Chain("d", 2, 0, HALF)

    def zed(dz):
        return (z + dz) % 8

    ways = ((0, up, 1), (1, down, -1))

    def ring_send(step, way, kind):
        device, sign = ways[way][1:]
        mine = terms.at[zed(sign * (4 - step) + 8), kind]
        copies.start("z%d%d%d" % (step, way, kind), mine, ring_in.at[step, way, kind], device)

    def ring_begin():
        ring_send(0, 0, 0)
        ring_send(0, 1, 1)
        ring_send(1, 0, 1)
        ring_send(1, 1, 0)

    def ring_step(step, kind, both=True):
        for way, device, sign in ways:
            if not both and way != kind:
                continue
            here = ring_in.at[step - 1, way, kind]
            copies.arrived("z%d%d%d" % (step - 1, way, kind), here, device)
            mine = zed(sign * (4 - step) + 8)
            terms[mine, kind] = (terms[mine, kind].astype(F32) + here[...].astype(F32)).astype(BF16)
            ring_send(step, way, kind)

    def ring_end(kind):
        total = terms[z, kind].astype(F32)
        for way, device, sign in ways:
            here = ring_in.at[3, way, kind]
            copies.arrived("z3%d%d" % (way, kind), here, device)
            total = total + here[...].astype(F32)
        side_out[kind] = total.T.reshape(2, HALF, 256)
        side_in[1, kind] = side_out[kind, 1 - y_lo].astype(BF16)
        copies.start("side%d" % kind, side_in.at[1, kind], side_in.at[0, kind], side)

    process(0, 0)
    gather_lift.near()
    gather_cot.other_far()
    gather_lift.other()
    gather_lift.near_rest()
    process(3, 0)
    process(1, 0)
    gather_lift.far()
    cores(0, 0)
    cores(3, 0)
    cores(1, 0)
    gather_lift.other_near()
    process(2, 0)
    process(0, 1)
    cores(2, 0)
    here_low.begin()
    gradients(0, 4)
    gather_lift.other_rest()
    cores(0, 1)
    process(1, 1)
    process(3, 1)
    here_low.next()
    cores(1, 1)
    cores(3, 1)
    gradients(4, 7)
    gather_lift.other_far()
    process(2, 1)
    gradients(7, 8)
    ring_begin()
    cores(2, 1)
    away.begin()
    from_across(0)
    from_across(1)
    from_across(3)
    ring_step(1, 0, False)
    ring_step(1, 1, False)
    away.next()
    from_across(2)
    here_high.begin()
    ring_step(2, 0)
    ring_step(2, 1)
    near_total = here_low.end()
    part[place(0, 1), 0, lower, :] = away.end().astype(BF16)
    copies.start("pair", part.at[place(0, 1), 0, lower], pair_in, across)
    here_high.next()
    ring_step(3, 0)
    ring_step(3, 1)
    ring_end(0)
    copies.arrived("pair", pair_in, across)
    back[lower, :] = (
        coarse[lower, :].astype(F32) + near_total + pair_in[...].astype(F32)
    ).astype(BF16)
    back[upper, :] = (coarse[upper, :].astype(F32) + here_high.end()).astype(BF16)
    ring_end(1)

    for q in range(4):
        raised = matmul(back[...], expand_ref[:, q * D1 : (q + 1) * D1])
        cells = pl.ds(q % 2, COLS // 2, stride=2)
        for c in range(4):
            block = raised[:, c * 128 : (c + 1) * 128].reshape(ROWS // 2, COLS // 2, 128)
            level[:, q // 2, c, cells, :] = level[:, q // 2, c, cells, :] + block

    @pl.loop(0, ROWS // 2)
    def _(r):
        for i in range(2):
            for c in range(4):
                prediction_ref[2 * r + i, :, c * 128 : (c + 1) * 128] = level[r, i, c].astype(BF16)

    for kind, out in ((0, grad_inner_ref), (1, grad_outer_ref)):
        copies.arrived("side%d" % kind, side_in.at[0, kind], side)
        out[...] = side_out[kind, y_lo] + side_in[0, kind].astype(F32)
    copies.finish()


def local(
    features, land_mask, land_embed, window_shift, fine_gain, qkv_weight, bias_table, mix_weight,
    merge_gain, merge_weight, coarse_gain, inner_weight, outer_weight, expand_weight, cotangent,
):
    vmem = pl.BlockSpec(memory_space=pltpu.VMEM)
    smem = pl.BlockSpec(memory_space=pltpu.SMEM)
    anywhere = pl.BlockSpec(memory_space=pl.ANY)
    wide_block = pltpu.VMEM((8, 2, CELLS, D2), BF16)
    prediction, grad_inner, grad_outer = pl.pallas_call(
        window_kernel,
        out_shape=(
            jax.ShapeDtypeStruct((ROWS, COLS, D1), BF16),
            jax.ShapeDtypeStruct((HALF, 256), F32),
            jax.ShapeDtypeStruct((HALF, 256), F32),
        ),
        in_specs=[smem] + [vmem] * 8 + [anywhere] * 6,
        out_specs=(vmem,) * 3,
        scratch_shapes=[
            pltpu.VMEM((D1, 3 * D1), BF16),
            pltpu.VMEM((D1, D1), BF16),
            pltpu.VMEM((4 * D1, D2), BF16),
            pltpu.VMEM((D2, 256), BF16),
            pltpu.VMEM((256, D2), BF16),
            pltpu.VMEM((D2, 4 * D1), BF16),
            pltpu.VMEM((HEADS1, 512), F32),
            pltpu.VMEM((2 * WH - 1, HEADS1, 128), F32),
            pltpu.VMEM((ROWS, COLS, D1), F32),
            pltpu.VMEM((ROWS, COLS, D1), BF16),
            pltpu.VMEM((2, ROWS, WL, D1), BF16),
            pltpu.VMEM((ROWS, COLS + 2 * WL, D1), F32),
            pltpu.VMEM((HEADS1, CELLS, CELLS), F32),
            pltpu.VMEM((ROWS, WL, D1), BF16),
            pltpu.VMEM((ROWS * WL, 3 * D1), BF16),
            pltpu.VMEM((ROWS, COLS + WL, D1), F32),
            pltpu.VMEM((ROWS, COLS, D1), BF16),
            pltpu.VMEM((ROWS // 2, 2, 4, COLS, 128), F32),
            pltpu.VMEM((CELLS, 4 * D1), BF16),
            pltpu.VMEM((CELLS, D2), BF16),
            pltpu.VMEM((CELLS, D2), BF16),
            wide_block,
            wide_block,
            wide_block,
            pltpu.VMEM((8, CELLS, D2), BF16),
            pltpu.VMEM((4, HALF, D2), BF16),
            pltpu.VMEM((3, 2, QUART, D2), BF16),
            pltpu.VMEM((3, 2, HALF, D2), BF16),
            pltpu.VMEM((HALF, D2), BF16),
            pltpu.VMEM((256, 16 * CELLS), BF16),
            pltpu.VMEM((256, 16 * CELLS), BF16),
            pltpu.VMEM((2, 256, D2), F32),
            pltpu.VMEM((8, 2, 256, 128), BF16),
            pltpu.VMEM((4, 2, 2, 256, 128), BF16),
            pltpu.VMEM((2, 2, HALF, 256), F32),
            pltpu.VMEM((2, 2, HALF, 256), BF16),
            pltpu.SemaphoreType.DMA((6,)),
            pltpu.SemaphoreType.DMA((COPIES,)),
            pltpu.SemaphoreType.DMA((COPIES,)),
        ],
        compiler_params=pltpu.CompilerParams(
            collective_id=0, has_side_effects=True, vmem_limit_bytes=46 * 1024 * 1024
        ),
        name="window",
    )(
        window_shift, features, land_mask, land_embed[None], fine_gain[None], bias_table,
        merge_gain[None], coarse_gain[None], cotangent,
        qkv_weight, mix_weight, merge_weight, inner_weight, outer_weight, expand_weight,
    )
    return prediction, grad_inner, grad_outer.T


def solution(mesh):
    return jax.shard_map(
        local,
        mesh=mesh,
        in_specs=(
            P("lat", "lon", None),
            P("lat", "lon"),
            P(),
            P(),
            P(),
            P(),
            P(),
            P(),
            P(),
            P(),
            P(),
            P(None, "lon"),
            P("lon", None),
            P(),
            P("lat", "lon", None),
        ),
        out_specs=(P("lat", "lon", None), P("lat", "lon"), P("lon", "lat")),
        check_vma=False,
    )
```

```python
import jax
import jax.numpy as jnp
from jax import lax
from jax.experimental import pallas as pl
from jax.experimental.pallas import tpu as pltpu
from jax.sharding import PartitionSpec as P

HEADS1 = 8
WH = 8
WL = 16
D1 = 512
D2 = 1024
ROWS = 16
COLS = 32
CELLS = 128
HALF = 64
COPIES = 72
HIDDEN = 512

NORM_EPS = 1e-05
GELU_SCALE = 0.7978845608028654
MESH = pl.DeviceIdType.MESH
BF16 = jnp.bfloat16
F32 = jnp.float32
LAST = (((1,), (1,)), ((), ()))


def normalise(values):
    centre = jnp.mean(values, axis=-1, keepdims=True)
    centred = values - centre
    spread = jnp.mean(centred * centred, axis=-1, keepdims=True)
    return centred * lax.rsqrt(spread + NORM_EPS)


def gelu_pair(pre_act):
    square = pre_act * pre_act
    inner = GELU_SCALE * (pre_act + 0.044715 * square * pre_act)
    tangent = jnp.tanh(inner)
    half = 0.5 * (1.0 + tangent)
    value = pre_act * half
    slope = half + value * (1.0 - tangent) * (GELU_SCALE + (3.0 * 0.044715 * GELU_SCALE) * square)
    return (value, slope)


def matmul(a, b):
    return jnp.dot(a, b, preferred_element_type=F32)


def matmul_t(a, b):
    return lax.dot_general(a, b, LAST, preferred_element_type=F32)


class Copies:
    def __init__(self, send_sems, recv_sems):
        self.send_sems, self.recv_sems = send_sems, recv_sems
        self.places, self.started = {}, []

    def describe(self, name, src, dst, device):
        place = self.places.setdefault(name, len(self.places))
        return pltpu.make_async_remote_copy(
            src_ref=src,
            dst_ref=dst,
            send_sem=self.send_sems.at[place],
            recv_sem=self.recv_sems.at[place],
            device_id=device,
            device_id_type=MESH,
        )

    def start(self, name, src, dst, device):
        copy = self.describe(name, src, dst, device)
        copy.start()
        self.started.append(copy)

    def arrived(self, name, dst, device):
        self.describe(name, dst, dst, device).wait_recv()

    def finish(self):
        for copy in self.started:
            copy.wait_send()


def window_kernel(
    shift_ref, mask_ref, embed_ref, fine_gain_ref, table_ref, merge_gain_ref,
    coarse_gain_ref,
    features_hbm, cotangent_hbm, qkv_hbm, mix_hbm, merge_hbm, inner_hbm, outer_hbm, expand_hbm,
    prediction_ref, grad_inner_ref, grad_outer_ref,
    features_ref, cotangent_ref, qkv_ref, mix_ref, merge_ref, inner_ref, outer_ref, expand_ref,
    padded, table_rows, base, normed, halo, wide, bias, window, projected, attended, shifted, level, merged, coarse, back,
    lift, cots, part, core_in, x_in,
    hidden, slopes, hidden_t, cot_pre_t, sums, terms, y_in, ring_in, pair_in, side_out, side_in,
    load_sems, send_sems, recv_sems,
):
    lon, lat = lax.axis_index("lon"), lax.axis_index("lat")
    core, y_hi, x = lon % 2, (lon // 2) % 2, lon // 4
    z, y_lo = lat // 2, lat % 2
    east, west = {"lon": (lon + 1) % 16}, {"lon": (lon + 15) % 16}
    partner = {"lon": lon + 1 - 2 * core}
    across = {"lon": lon + 2 - 4 * y_hi}
    right, left = {"lon": (lon + 4) % 16}, {"lon": (lon + 12) % 16}
    opposite = {"lon": (lon + 8) % 16}
    up, down = {"lat": (lat + 2) % 16}, {"lat": (lat + 14) % 16}
    side = {"lat": lat + 1 - 2 * y_lo}

    loads, slots = {}, iter(range(12))

    def load(name, src, dst):
        loads[name] = pltpu.make_async_copy(src, dst, load_sems.at[next(slots)])
        loads[name].start()

    own = pl.ds(0, HIDDEN // 2)
    other = pl.ds(HIDDEN // 2, HIDDEN // 2)
    load("features", features_hbm, features_ref)
    load("cotangent", cotangent_hbm, cotangent_ref)
    for j in range(4):
        rows = pl.ds(j * 256, 256)
        load("expand%d" % j, expand_hbm.at[rows], expand_ref.at[rows])
    barrier = pltpu.get_barrier_semaphore()
    neighbours = (east, west, partner, across, right, left, opposite, up, down, side)
    for device in neighbours:
        pl.semaphore_signal(barrier, inc=1, device_id=device, device_id_type=MESH)

    loads["features"].wait()
    pl.semaphore_wait(barrier, len(neighbours))
    copies = Copies(send_sems, recv_sems)
    early, late = pl.ds(0, 256), pl.ds(256, D2 - 256)
    copies.start("inner0", inner_hbm.at[early], inner_ref.at[1, early], across)

    diagonal = lax.broadcasted_iota(jnp.int32, (COLS, COLS), 0) == lax.broadcasted_iota(
        jnp.int32, (COLS, COLS), 1
    )

    @pl.loop(0, ROWS, unroll=4)
    def _(r):
        land = mask_ref[pl.ds(r, 1), :].astype(F32)
        land = jnp.sum(jnp.where(diagonal, land, 0.0), axis=1, keepdims=True)
        cells = features_ref[r].astype(F32) + land * embed_ref[...]
        base[r] = cells
        rounded = (normalise(cells) * fine_gain_ref[...]).astype(BF16)
        normed[r] = rounded
        wide[r, WL : WL + COLS, :] = rounded.astype(F32)

    copies.start("halo e", normed.at[:, pl.ds(COLS - WL, WL), :], halo.at[0], east)
    copies.start("halo w", normed.at[:, pl.ds(0, WL), :], halo.at[1], west)

    padded[...] = jnp.zeros_like(padded)
    padded[:, 0 : table_ref.shape[1]] = table_ref[...]
    offsets = padded[...]
    top = offsets.astype(BF16)
    rest = offsets - top.astype(F32)
    middle = rest.astype(BF16)
    bottom = (rest - middle.astype(F32)).astype(BF16)
    turn = lax.broadcasted_iota(jnp.int32, (512, 640), 0) + lax.broadcasted_iota(
        jnp.int32, (512, 640), 1
    )
    turn = jnp.where(turn == table_ref.shape[1] - 1, 1.0, 0.0).astype(BF16)
    flipped = matmul(top, turn) + matmul(middle, turn) + matmul(bottom, turn)
    for i in range(2 * WH - 1):
        start = i * (2 * WL - 1)
        table_rows[i] = flipped[:, start : start + 128]
    lane = lax.broadcasted_iota(jnp.int32, (WL, 128), 1)

    @pl.loop(0, HEADS1)
    def _(h):
        halves = []
        for k in range(2):
            total = jnp.zeros((WL, 128), F32)
            for i in range(8 if k == 0 else 7):
                row = jnp.broadcast_to(table_rows[8 * k + i, pl.ds(h, 1), :], (WL, 128))
                turned = pltpu.roll(row, (128 - 15 + 16 * i) % 128, 1, stride=1, stride_axis=0)
                total = jnp.where(lane // 16 == i, turned, total)
            halves.append(total)
        both = jnp.concatenate(halves, axis=1)
        for i in range(WH):
            start = (WH - 1 - i) * WL
            bias[h, i * WL : (i + 1) * WL, :] = both[:, start : start + 128]

    def place(dx):
        return (0, 1, 3, 2)[dx % 4]

    def fold(store):
        @pl.loop(0, ROWS // 2, unroll=4)
        def _(r):
            store(
                r,
                [
                    jnp.concatenate(
                        [level[r, i, c, pl.ds(j, COLS // 2, stride=2), :] for c in range(4)], axis=1
                    )
                    for i in range(2)
                    for j in range(2)
                ],
            )

    loads["cotangent"].wait()

    @pl.loop(0, ROWS // 2)
    def _(r):
        for i in range(2):
            cells = cotangent_ref[2 * r + i].astype(F32)
            for c in range(4):
                level[r, i, c] = cells[:, c * 128 : (c + 1) * 128]

    def store_cot(r, quads):
        rows = pl.ds(pl.multiple_of(r * 16, 16), 16)
        for q in range(4):
            merged[rows, q * D1 : (q + 1) * D1] = quads[q].astype(BF16)

    fold(store_cot)
    for j in range(4):
        lanes = slice(j * 256, (j + 1) * 256)
        loads["expand%d" % j].wait()
        if j == 2:
            load("qkv", qkv_hbm, qkv_ref)
        cots[0, 0, :, lanes] = matmul_t(merged[...], expand_ref[lanes, :]).astype(BF16)

    load("mix", mix_hbm, mix_ref)
    load("merge", merge_hbm, merge_ref)
    load("inner", inner_hbm, inner_ref.at[0])
    load("outer", outer_hbm, outer_ref.at[own])

    front, rear = pl.ds(0, HALF), pl.ds(HALF, HALF)
    moves = {"r": (right, -1, 0), "l": (left, 1, 0), "o": (opposite, 2, 0), "p": (partner, 0, 1)}

    class Gather:
        def __init__(self, name, array):
            self.name, self.array = name, array

        def at(self, dx, rows=None, dk=0):
            block = self.array.at[place(dx), dk]
            return block if rows is None else block.at[rows]

        def send(self, name, dx, rows, way):
            device, mx, mk = moves[way]
            copies.start(self.name + name, self.at(dx, rows), self.at(dx + mx, rows, mk), device)

        def came(self, name, dx, rows, way):
            copies.arrived(self.name + name, self.at(dx, rows), moves[way][0])

        def share(self, dx):
            self.send("p%d" % dx, dx, None, "p")

        def shared(self, dx):
            copies.arrived(self.name + "p%d" % dx, self.at(dx, None, 1), partner)

    gather_cot, gather_lift = Gather("c", cots), Gather("l", lift)
    gather_cot.send("r", 0, None, "r")
    gather_cot.send("l", 0, None, "l")
    gather_cot.send("o", 0, None, "o")
    gather_cot.share(0)

    offset = shift_ref[0]
    first_head = lax.broadcasted_iota(jnp.int32, (CELLS, 128), 1) < 64
    ones = jnp.ones((CELLS, 128), BF16)

    def attend(w):
        @pl.loop(0, ROWS, unroll=4)
        def _(r):
            cells = wide[r, w * WL : (w + 2) * WL, :]
            window[r] = pltpu.roll(cells, 2 * WL - offset, 0)[:WL].astype(BF16)

        @pl.loop(0, 6, unroll=3)
        def _(j):
            lanes = pl.ds(pl.multiple_of(j * 256, 256), 256)
            rows = window[...].reshape(ROWS * WL, D1)
            projected[:, lanes] = matmul(rows, qkv_ref[:, lanes]).astype(BF16)

        @pl.loop(0, 8, unroll=8)
        def _(k):
            band, pair = k // 4, k % 4
            rows = pl.ds(pl.multiple_of(band * CELLS, CELLS), CELLS)

            def lanes(kind):
                return pl.ds(pl.multiple_of(kind * D1 + pair * 128, 128), 128)

            queries = projected[rows, lanes(0)] * 0.125
            zero = jnp.zeros_like(queries)
            queries = jnp.concatenate(
                [jnp.where(first_head, queries, zero), jnp.where(first_head, zero, queries)], axis=0
            )
            scores = matmul_t(queries, projected[rows, lanes(1)])
            scores = scores + bias[pl.ds(2 * pair, 2)].reshape(2 * CELLS, 128)
            expo = jnp.exp(scores - jnp.max(scores, axis=1, keepdims=True)).astype(BF16)
            values = jnp.concatenate([projected[rows, lanes(2)], ones], axis=1)
            sums = matmul(expo, values)
            heads = jnp.where(first_head, sums[:CELLS, :128], sums[CELLS:, :128]) / jnp.where(
                first_head, sums[:CELLS, 128:], sums[CELLS:, 128:]
            )
            attended[pl.ds(band * WH, WH), w * WL : (w + 1) * WL, lanes(0)] = heads.reshape(
                WH, WL, 128
            )

    loads["qkv"].wait()
    attend(1)
    copies.arrived("halo e", halo.at[0], east)
    copies.arrived("halo w", halo.at[1], west)

    @pl.loop(0, ROWS)
    def _(r):
        wide[r, 0:WL, :] = halo[0, r].astype(F32)
        wide[r, WL + COLS :, :] = halo[1, r].astype(F32)

    copies.start("inner1", inner_hbm.at[late], inner_ref.at[1, late], across)
    attend(0)
    attend(2)
    copies.start("outer", outer_hbm, outer_ref.at[other], across)

    loads["mix"].wait()

    @pl.loop(0, ROWS, unroll=4)
    def _(r):
        shifted[r] = pltpu.roll(attended[r], COLS + offset, 0)[:COLS].astype(BF16)

    @pl.loop(0, 2)
    def _(i):
        rows = pl.ds(i * 8, 8)
        mixed = matmul(shifted[rows].reshape(2 * CELLS, D1), mix_ref[...]).reshape(8, COLS, D1)
        mixed = (base[rows] + mixed).astype(BF16).astype(F32).reshape(4, 2, COLS, D1)
        for c in range(4):
            level[pl.ds(i * 4, 4), :, c] = mixed[..., c * 128 : (c + 1) * 128]

    def store_merged(r, quads):
        centre = sum(jnp.sum(quad, axis=1, keepdims=True) for quad in quads) / (4 * D1)
        quads = [quad - centre for quad in quads]
        spread = sum(jnp.sum(quad * quad, axis=1, keepdims=True) for quad in quads) / (4 * D1)
        scale = lax.rsqrt(spread + NORM_EPS)
        rows = pl.ds(pl.multiple_of(r * 16, 16), 16)
        for q in range(4):
            lanes = slice(q * D1, (q + 1) * D1)
            merged[rows, lanes] = (quads[q] * scale * merge_gain_ref[:, lanes]).astype(BF16)

    fold(store_merged)
    loads["merge"].wait()

    @pl.loop(0, 4)
    def _(j):
        lanes = pl.ds(pl.multiple_of(j * 256, 256), 256)
        coarse[:, lanes] = matmul(merged[...], merge_ref[:, lanes]).astype(BF16)

    @pl.loop(0, 4, unroll=4)
    def _(i):
        rows = pl.ds(pl.multiple_of(i * 32, 32), 32)
        lift[0, 0, rows, :] = (
            normalise(coarse[rows, :].astype(F32)) * coarse_gain_ref[...]
        ).astype(BF16)

    gather_lift.send("r0", 0, front, "r")
    gather_lift.send("l0", 0, rear, "l")
    gather_lift.send("r1", 0, rear, "r")
    gather_lift.send("l1", 0, front, "l")
    gather_lift.share(0)
    for way, dx in (("r", 3), ("l", 1), ("o", 2)):
        gather_cot.came(way, dx, None, way)
        gather_cot.share(dx)
    copies.arrived("inner0", inner_ref.at[1, early], across)
    copies.arrived("inner1", inner_ref.at[1, late], across)
    loads["inner"].wait()
    loads["outer"].wait()

    unit = lax.broadcasted_iota(jnp.int32, (256, 256), 0) == lax.broadcasted_iota(
        jnp.int32, (256, 256), 1
    )
    unit = jnp.where(unit, 1.0, 0.0).astype(BF16)

    def activate(dx):
        gather_lift.shared(dx)
        p = place(dx)
        columns = slice(p * 2 * CELLS, (p + 1) * 2 * CELLS)
        for half in range(2):
            rows = slice(half * 256, (half + 1) * 256)
            pre = matmul(lift[p].reshape(2 * CELLS, D2), inner_ref[half])
            value, slope = gelu_pair(pre)
            value = value.astype(BF16)
            hidden[p, :, rows] = value
            slopes[p, half] = slope
            hidden_t[rows, columns] = matmul_t(unit, value).astype(BF16)

    def project(dx):
        p = place(dx)
        part[p] = matmul(hidden[p], outer_ref[...]).astype(BF16).reshape(2, CELLS, D2)
        copies.start("s%d" % dx, part.at[p, 1], core_in.at[p], partner)

    def pull_back(dx):
        p = place(dx)
        columns = slice(p * 2 * CELLS, (p + 1) * 2 * CELLS)
        for half in range(2):
            rows = slice(half * 256, (half + 1) * 256)
            cot_hidden = matmul_t(cots[p].reshape(2 * CELLS, D2), outer_ref[rows, :])
            cot_pre = (cot_hidden * slopes[p, half]).astype(BF16)
            cot_pre_t[rows, columns] = matmul_t(unit, cot_pre).astype(BF16)

    def gradient(kind, begin, end):
        rows, array = ((cot_pre_t, lift), (hidden_t, cots))[kind]

        @pl.loop(0, 4)
        def _(j):
            lanes = pl.ds(pl.multiple_of(j * 256, 256), 256)
            cells = array[begin:end, :, :, lanes].reshape((end - begin) * 2 * CELLS, 256)
            term = matmul(rows[:, begin * 2 * CELLS : end * 2 * CELLS], cells)
            if begin > 0:
                term = term + sums[:, lanes]
            if end < 4:
                sums[:, lanes] = term
            else:
                for k in range(2):
                    half = term[:, k * 128 : (k + 1) * 128].astype(BF16)
                    terms[2 * j + k, kind] = half.reshape(2, 256, 128)

    def cores(dx):
        p = place(dx)
        copies.arrived("s%d" % dx, core_in.at[p], partner)
        part[p, 0] = (part[p, 0].astype(F32) + core_in[p].astype(F32)).astype(BF16)
        if dx > 0:
            device = {1: right, 3: left, 2: opposite}[dx]
            copies.start("t%d" % dx, part.at[p, 0], x_in.at[dx - 1], device)

    def zed(dz):
        return (z + dz) % 8

    ways = ((0, up, 1), (1, down, -1))
    thin = (pl.ds(0, 128), pl.ds(128, 128))

    def term_of(mine, chain):
        if chain < 2:
            return terms.at[mine, 1, chain]
        return terms.at[mine, 0, 0, thin[chain - 2]]

    def landing(step, way, chain):
        if chain < 2:
            return ring_in.at[step, way, 0, chain]
        return ring_in.at[step, way, 1, 0, thin[chain - 2]]

    def ring_send(step, way, chain):
        device, sign = ways[way][1:]
        mine = zed(sign * (4 - step) + 8)
        name = "z%d%d%d" % (step, way, chain)
        copies.start(name, term_of(mine, chain), landing(step, way, chain), device)

    def ring_begin(chain):
        ring_send(0, chain % 2, chain)

    def ring_other(chain):
        ring_send(1, 1 - chain % 2, chain)

    def ring_take(step, way, chain):
        here = landing(step, way, chain)
        copies.arrived("z%d%d%d" % (step, way, chain), here, ways[way][1])
        return here[...].astype(F32)

    def ring_step(step, chain):
        for way, device, sign in ways:
            if step == 1 and way != chain % 2:
                continue
            mine = term_of(zed(sign * (4 - step) + 8), chain)
            mine[...] = (mine[...].astype(F32) + ring_take(step - 1, way, chain)).astype(BF16)
            ring_send(step, way, chain)

    def ring_end(chain):
        total = term_of(z, chain)[...].astype(F32)
        return total + ring_take(3, 0, chain) + ring_take(3, 1, chain)

    order = (4, 3, 5, 2, 6, 1, 7, 0)

    def pair_begin():
        for d in order:
            copies.start("y%d" % d, terms.at[zed(d), 0, 1], y_in.at[d], across)

    def pair_add(d):
        copies.arrived("y%d" % d, y_in.at[d], across)
        mine = zed(d)
        terms[mine, 0, 0] = (terms[mine, 0, 0].astype(F32) + y_in[d].astype(F32)).astype(BF16)

    def side_begin(kind, total):
        side_out[kind] = total.T.reshape(2, HALF, 256)
        side_in[1, kind] = side_out[kind, 1 - y_lo].astype(BF16)
        copies.start("side%d" % kind, side_in.at[1, kind], side_in.at[0, kind], side)

    activate(0)
    for name, rows, dx, way in (("r0", front, 3, "r"), ("l0", rear, 1, "l")):
        gather_lift.came(name, dx, rows, way)
        gather_lift.send("f" + way, dx, rows, way)
    gather_lift.came("r1", 3, rear, "r")
    gather_lift.share(3)
    gather_lift.came("l1", 1, front, "l")
    gather_lift.share(1)
    activate(3)
    activate(1)
    for dx in (0, 3, 1, 2):
        gather_cot.shared(dx)
    gradient(1, 0, 3)
    gather_lift.came("fr", 2, front, "r")
    gather_lift.came("fl", 2, rear, "l")
    gather_lift.share(2)
    activate(2)
    gradient(1, 3, 4)
    ring_begin(0)
    ring_begin(1)
    ring_other(0)
    ring_other(1)
    copies.arrived("outer", outer_ref.at[other], across)
    project(2)
    project(3)
    project(1)
    project(0)
    cores(2)
    cores(3)
    cores(1)
    pull_back(0)
    pull_back(3)
    ring_step(1, 0)
    ring_step(1, 1)
    pull_back(1)
    pull_back(2)
    gradient(0, 0, 4)
    pair_begin()
    cores(0)
    ring_step(2, 0)
    ring_step(2, 1)
    pair_add(4)
    ring_begin(2)
    ring_begin(3)
    pair_add(3)
    pair_add(5)
    ring_other(2)
    ring_other(3)
    ring_step(3, 0)
    ring_step(3, 1)
    ring_step(1, 2)
    ring_step(1, 3)
    pair_add(2)
    pair_add(6)
    ring_step(2, 2)
    ring_step(2, 3)
    pair_in[1] = ring_end(1).astype(BF16)
    copies.start("pair", pair_in.at[1], pair_in.at[0], across)
    outer_total = ring_end(0)
    pair_add(1)
    pair_add(7)
    ring_step(3, 2)
    ring_step(3, 3)
    copies.arrived("pair", pair_in.at[0], across)
    side_begin(1, outer_total + pair_in[0].astype(F32))
    pair_add(0)

    update = part[0, 0].astype(F32)
    for dx, device in ((1, right), (3, left), (2, opposite)):
        copies.arrived("t%d" % dx, x_in.at[dx - 1], device)
        update = update + x_in[dx - 1].astype(F32)
    back[...] = (coarse[...].astype(F32) + update).astype(BF16)

    for q in range(4):
        raised = matmul(back[...], expand_ref[:, q * D1 : (q + 1) * D1])
        cells = pl.ds(q % 2, COLS // 2, stride=2)
        for c in range(4):
            block = raised[:, c * 128 : (c + 1) * 128].reshape(ROWS // 2, COLS // 2, 128)
            level[:, q // 2, c, cells, :] = level[:, q // 2, c, cells, :] + block

    @pl.loop(0, ROWS // 2)
    def _(r):
        for i in range(2):
            for c in range(4):
                prediction_ref[2 * r + i, :, c * 128 : (c + 1) * 128] = level[r, i, c].astype(BF16)

    side_begin(0, jnp.concatenate([ring_end(2), ring_end(3)], axis=0))
    for kind, out in ((1, grad_outer_ref), (0, grad_inner_ref)):
        copies.arrived("side%d" % kind, side_in.at[0, kind], side)
        out[...] = side_out[kind, y_lo] + side_in[0, kind].astype(F32)
    copies.finish()


def hand_over_kernel(*refs):
    for k in range(3):
        refs[3 + k][...] = refs[k][...]


def local(
    features, land_mask, land_embed, window_shift, fine_gain, qkv_weight, bias_table, mix_weight,
    merge_gain, merge_weight, coarse_gain, inner_weight, outer_weight, expand_weight, cotangent,
):
    vmem = pl.BlockSpec(memory_space=pltpu.VMEM)
    smem = pl.BlockSpec(memory_space=pltpu.SMEM)
    anywhere = pl.BlockSpec(memory_space=pl.ANY)
    wide_block = pltpu.VMEM((4, 2, CELLS, D2), BF16)
    outputs = pl.pallas_call(
        window_kernel,
        out_shape=(
            jax.ShapeDtypeStruct((ROWS, COLS, D1), BF16),
            jax.ShapeDtypeStruct((HALF, 256), F32),
            jax.ShapeDtypeStruct((HALF, 256), F32),
        ),
        in_specs=[smem] + [vmem] * 6 + [anywhere] * 8,
        out_specs=(vmem,) * 3,
        scratch_shapes=[
            pltpu.VMEM((ROWS, COLS, D1), BF16),
            pltpu.VMEM((ROWS, COLS, D1), BF16),
            pltpu.VMEM((D1, 3 * D1), BF16),
            pltpu.VMEM((D1, D1), BF16),
            pltpu.VMEM((4 * D1, D2), BF16),
            pltpu.VMEM((2, D2, HIDDEN // 2), BF16),
            pltpu.VMEM((HIDDEN, D2), BF16),
            pltpu.VMEM((D2, 4 * D1), BF16),
            pltpu.VMEM((HEADS1, 512), F32),
            pltpu.VMEM((2 * WH - 1, HEADS1, 128), F32),
            pltpu.VMEM((ROWS, COLS, D1), F32),
            pltpu.VMEM((ROWS, COLS, D1), BF16),
            pltpu.VMEM((2, ROWS, WL, D1), BF16),
            pltpu.VMEM((ROWS, COLS + 2 * WL, D1), F32),
            pltpu.VMEM((HEADS1, CELLS, CELLS), F32),
            pltpu.VMEM((ROWS, WL, D1), BF16),
            pltpu.VMEM((ROWS * WL, 3 * D1), BF16),
            pltpu.VMEM((ROWS, COLS + WL, D1), F32),
            pltpu.VMEM((ROWS, COLS, D1), BF16),
            pltpu.VMEM((ROWS // 2, 2, 4, COLS, 128), F32),
            pltpu.VMEM((CELLS, 4 * D1), BF16),
            pltpu.VMEM((CELLS, D2), BF16),
            pltpu.VMEM((CELLS, D2), BF16),
            wide_block,
            wide_block,
            wide_block,
            pltpu.VMEM((4, CELLS, D2), BF16),
            pltpu.VMEM((3, CELLS, D2), BF16),
            pltpu.VMEM((4, 2 * CELLS, HIDDEN), BF16),
            pltpu.VMEM((4, 2, 2 * CELLS, 256), F32),
            pltpu.VMEM((HIDDEN, 8 * CELLS), BF16),
            pltpu.VMEM((HIDDEN, 8 * CELLS), BF16),
            pltpu.VMEM((HIDDEN, D2), F32),
            pltpu.VMEM((8, 2, 2, 256, 128), BF16),
            pltpu.VMEM((8, 256, 128), BF16),
            pltpu.VMEM((4, 2, 2, 2, 256, 128), BF16),
            pltpu.VMEM((2, 256, 128), BF16),
            pltpu.VMEM((2, 2, HALF, 256), F32),
            pltpu.VMEM((2, 2, HALF, 256), BF16),
            pltpu.SemaphoreType.DMA((12,)),
            pltpu.SemaphoreType.DMA((COPIES,)),
            pltpu.SemaphoreType.DMA((COPIES,)),
        ],
        compiler_params=pltpu.CompilerParams(
            collective_id=0, has_side_effects=True, vmem_limit_bytes=56 * 1024 * 1024
        ),
        name="window",
    )(
        window_shift, land_mask, land_embed[None], fine_gain[None], bias_table,
        merge_gain[None], coarse_gain[None], features, cotangent,
        qkv_weight, mix_weight, merge_weight, inner_weight, outer_weight, expand_weight,
    )
    prediction, grad_inner, grad_outer = pl.pallas_call(
        hand_over_kernel,
        out_shape=tuple(jax.ShapeDtypeStruct(x.shape, x.dtype) for x in outputs),
        in_specs=[vmem] * 3,
        out_specs=(vmem,) * 3,
        name="hand_over",
    )(*outputs)
    return prediction, grad_inner, grad_outer.T


def solution(mesh):
    return jax.shard_map(
        local,
        mesh=mesh,
        in_specs=(
            P("lat", "lon", None),
            P("lat", "lon"),
            P(),
            P(),
            P(),
            P(),
            P(),
            P(),
            P(),
            P(),
            P(),
            P(None, "lon"),
            P("lon", None),
            P(),
            P("lat", "lon", None),
        ),
        out_specs=(P("lat", "lon", None), P("lat", "lon"), P("lon", "lat")),
        check_vma=False,
    )
```

```python
import jax
import jax.numpy as jnp
from jax import lax
from jax.experimental import pallas as pl
from jax.experimental.pallas import tpu as pltpu
from jax.sharding import PartitionSpec as P

HEADS1 = 8
WH = 8
WL = 16
D1 = 512
D2 = 1024
ROWS = 16
COLS = 32
CELLS = 128
HALF = 64
COPIES = 72
HIDDEN = 512

NORM_EPS = 1e-05
GELU_SCALE = 0.7978845608028654
MESH = pl.DeviceIdType.MESH
BF16 = jnp.bfloat16
F32 = jnp.float32
LAST = (((1,), (1,)), ((), ()))


def normalise(values):
    centre = jnp.mean(values, axis=-1, keepdims=True)
    centred = values - centre
    spread = jnp.mean(centred * centred, axis=-1, keepdims=True)
    return centred * lax.rsqrt(spread + NORM_EPS)


def gelu_pair(pre_act):
    square = pre_act * pre_act
    inner = GELU_SCALE * (pre_act + 0.044715 * square * pre_act)
    tangent = jnp.tanh(inner)
    half = 0.5 * (1.0 + tangent)
    value = pre_act * half
    slope = half + value * (1.0 - tangent) * (GELU_SCALE + (3.0 * 0.044715 * GELU_SCALE) * square)
    return (value, slope)


def matmul(a, b):
    return jnp.dot(a, b, preferred_element_type=F32)


def matmul_t(a, b):
    return lax.dot_general(a, b, LAST, preferred_element_type=F32)


class Copies:
    def __init__(self, send_sems, recv_sems):
        self.send_sems, self.recv_sems = send_sems, recv_sems
        self.places, self.started = {}, []

    def describe(self, name, src, dst, device):
        place = self.places.setdefault(name, len(self.places))
        return pltpu.make_async_remote_copy(
            src_ref=src,
            dst_ref=dst,
            send_sem=self.send_sems.at[place],
            recv_sem=self.recv_sems.at[place],
            device_id=device,
            device_id_type=MESH,
        )

    def start(self, name, src, dst, device):
        copy = self.describe(name, src, dst, device)
        copy.start()
        self.started.append(copy)

    def arrived(self, name, dst, device):
        self.describe(name, dst, dst, device).wait_recv()

    def finish(self):
        for copy in self.started:
            copy.wait_send()


def window_kernel(
    shift_ref, mask_ref, embed_ref, fine_gain_ref, table_ref, merge_gain_ref,
    coarse_gain_ref,
    features_hbm, cotangent_hbm, qkv_hbm, mix_hbm, merge_hbm, inner_hbm, outer_hbm, expand_hbm,
    prediction_ref, grad_inner_ref, grad_outer_ref,
    features_ref, cotangent_ref, qkv_ref, mix_ref, merge_ref, inner_ref, outer_ref, expand_ref,
    padded, table_rows, base, normed, halo, wide, bias, window, projected, attended, shifted, level, merged, coarse, back,
    lift, cots, part, core_in, x_in,
    hidden, slopes, hidden_t, cot_pre_t, sums, terms, y_in, ring_in, side_out, side_in, corner_out, corner_in,
    load_sems, send_sems, recv_sems,
):
    lon, lat = lax.axis_index("lon"), lax.axis_index("lat")
    core, y_hi, x = lon % 2, (lon // 2) % 2, lon // 4
    z, y_lo = lat // 2, lat % 2
    east, west = {"lon": (lon + 1) % 16}, {"lon": (lon + 15) % 16}
    partner = {"lon": lon + 1 - 2 * core}
    across = {"lon": lon + 2 - 4 * y_hi}
    right, left = {"lon": (lon + 4) % 16}, {"lon": (lon + 12) % 16}
    opposite = {"lon": (lon + 8) % 16}
    up, down = {"lat": (lat + 2) % 16}, {"lat": (lat + 14) % 16}
    side = {"lat": lat + 1 - 2 * y_lo}
    corner = {"lat": lat + 1 - 2 * y_lo, "lon": lon + 2 - 4 * y_hi}

    loads, slots = {}, iter(range(12))

    def load(name, src, dst):
        loads[name] = pltpu.make_async_copy(src, dst, load_sems.at[next(slots)])
        loads[name].start()

    own = pl.ds(0, HIDDEN // 2)
    other = pl.ds(HIDDEN // 2, HIDDEN // 2)
    load("features", features_hbm, features_ref)
    load("cotangent", cotangent_hbm, cotangent_ref)
    for j in range(4):
        rows = pl.ds(j * 256, 256)
        load("expand%d" % j, expand_hbm.at[rows], expand_ref.at[rows])
    barrier = pltpu.get_barrier_semaphore()
    neighbours = (east, west, partner, across, right, left, opposite, up, down, side, corner)
    for device in neighbours:
        pl.semaphore_signal(barrier, inc=1, device_id=device, device_id_type=MESH)

    loads["features"].wait()
    pl.semaphore_wait(barrier, len(neighbours))
    copies = Copies(send_sems, recv_sems)
    early, late = pl.ds(0, 256), pl.ds(256, D2 - 256)
    copies.start("inner0", inner_hbm.at[early], inner_ref.at[1, early], across)

    diagonal = lax.broadcasted_iota(jnp.int32, (COLS, COLS), 0) == lax.broadcasted_iota(
        jnp.int32, (COLS, COLS), 1
    )

    @pl.loop(0, ROWS, unroll=4)
    def _(r):
        land = mask_ref[pl.ds(r, 1), :].astype(F32)
        land = jnp.sum(jnp.where(diagonal, land, 0.0), axis=1, keepdims=True)
        cells = features_ref[r].astype(F32) + land * embed_ref[...]
        base[r] = cells
        rounded = (normalise(cells) * fine_gain_ref[...]).astype(BF16)
        normed[r] = rounded
        wide[r, WL : WL + COLS, :] = rounded.astype(F32)

    copies.start("halo e", normed.at[:, pl.ds(COLS - WL, WL), :], halo.at[0], east)
    copies.start("halo w", normed.at[:, pl.ds(0, WL), :], halo.at[1], west)

    padded[...] = jnp.zeros_like(padded)
    padded[:, 0 : table_ref.shape[1]] = table_ref[...]
    offsets = padded[...]
    top = offsets.astype(BF16)
    rest = offsets - top.astype(F32)
    middle = rest.astype(BF16)
    bottom = (rest - middle.astype(F32)).astype(BF16)
    turn = lax.broadcasted_iota(jnp.int32, (512, 640), 0) + lax.broadcasted_iota(
        jnp.int32, (512, 640), 1
    )
    turn = jnp.where(turn == table_ref.shape[1] - 1, 1.0, 0.0).astype(BF16)
    flipped = matmul(top, turn) + matmul(middle, turn) + matmul(bottom, turn)
    for i in range(2 * WH - 1):
        start = i * (2 * WL - 1)
        table_rows[i] = flipped[:, start : start + 128]
    lane = lax.broadcasted_iota(jnp.int32, (WL, 128), 1)

    @pl.loop(0, HEADS1)
    def _(h):
        halves = []
        for k in range(2):
            total = jnp.zeros((WL, 128), F32)
            for i in range(8 if k == 0 else 7):
                row = jnp.broadcast_to(table_rows[8 * k + i, pl.ds(h, 1), :], (WL, 128))
                turned = pltpu.roll(row, (128 - 15 + 16 * i) % 128, 1, stride=1, stride_axis=0)
                total = jnp.where(lane // 16 == i, turned, total)
            halves.append(total)
        both = jnp.concatenate(halves, axis=1)
        for i in range(WH):
            start = (WH - 1 - i) * WL
            bias[h, i * WL : (i + 1) * WL, :] = both[:, start : start + 128]

    def place(dx):
        return (0, 1, 3, 2)[dx % 4]

    def fold(store):
        @pl.loop(0, ROWS // 2, unroll=4)
        def _(r):
            store(
                r,
                [
                    jnp.concatenate(
                        [level[r, i, c, pl.ds(j, COLS // 2, stride=2), :] for c in range(4)], axis=1
                    )
                    for i in range(2)
                    for j in range(2)
                ],
            )

    loads["cotangent"].wait()

    @pl.loop(0, ROWS // 2)
    def _(r):
        for i in range(2):
            cells = cotangent_ref[2 * r + i].astype(F32)
            for c in range(4):
                level[r, i, c] = cells[:, c * 128 : (c + 1) * 128]

    def store_cot(r, quads):
        rows = pl.ds(pl.multiple_of(r * 16, 16), 16)
        for q in range(4):
            merged[rows, q * D1 : (q + 1) * D1] = quads[q].astype(BF16)

    fold(store_cot)
    for j in range(4):
        lanes = slice(j * 256, (j + 1) * 256)
        loads["expand%d" % j].wait()
        if j == 2:
            load("qkv", qkv_hbm, qkv_ref)
        cots[0, 0, :, lanes] = matmul_t(merged[...], expand_ref[lanes, :]).astype(BF16)

    load("mix", mix_hbm, mix_ref)
    load("merge", merge_hbm, merge_ref)
    load("inner", inner_hbm, inner_ref.at[0])
    load("outer", outer_hbm, outer_ref.at[own])

    front, rear = pl.ds(0, HALF), pl.ds(HALF, HALF)
    moves = {"r": (right, -1, 0), "l": (left, 1, 0), "o": (opposite, 2, 0), "p": (partner, 0, 1)}

    class Gather:
        def __init__(self, name, array):
            self.name, self.array = name, array

        def at(self, dx, rows=None, dk=0):
            block = self.array.at[place(dx), dk]
            return block if rows is None else block.at[rows]

        def send(self, name, dx, rows, way):
            device, mx, mk = moves[way]
            copies.start(self.name + name, self.at(dx, rows), self.at(dx + mx, rows, mk), device)

        def came(self, name, dx, rows, way):
            copies.arrived(self.name + name, self.at(dx, rows), moves[way][0])

        def share(self, dx):
            self.send("p%d" % dx, dx, None, "p")

        def shared(self, dx):
            copies.arrived(self.name + "p%d" % dx, self.at(dx, None, 1), partner)

    gather_cot, gather_lift = Gather("c", cots), Gather("l", lift)
    gather_cot.send("r", 0, None, "r")
    gather_cot.send("l", 0, None, "l")
    gather_cot.send("o", 0, None, "o")
    gather_cot.share(0)

    offset = shift_ref[0]
    first_head = lax.broadcasted_iota(jnp.int32, (CELLS, 128), 1) < 64
    ones = jnp.ones((CELLS, 128), BF16)

    def attend(w):
        @pl.loop(0, ROWS, unroll=4)
        def _(r):
            cells = wide[r, w * WL : (w + 2) * WL, :]
            window[r] = pltpu.roll(cells, 2 * WL - offset, 0)[:WL].astype(BF16)

        @pl.loop(0, 6, unroll=3)
        def _(j):
            lanes = pl.ds(pl.multiple_of(j * 256, 256), 256)
            rows = window[...].reshape(ROWS * WL, D1)
            projected[:, lanes] = matmul(rows, qkv_ref[:, lanes]).astype(BF16)

        @pl.loop(0, 8, unroll=8)
        def _(k):
            band, pair = k // 4, k % 4
            rows = pl.ds(pl.multiple_of(band * CELLS, CELLS), CELLS)

            def lanes(kind):
                return pl.ds(pl.multiple_of(kind * D1 + pair * 128, 128), 128)

            queries = projected[rows, lanes(0)] * 0.125
            zero = jnp.zeros_like(queries)
            queries = jnp.concatenate(
                [jnp.where(first_head, queries, zero), jnp.where(first_head, zero, queries)], axis=0
            )
            scores = matmul_t(queries, projected[rows, lanes(1)])
            scores = scores + bias[pl.ds(2 * pair, 2)].reshape(2 * CELLS, 128)
            expo = jnp.exp(scores - jnp.max(scores, axis=1, keepdims=True)).astype(BF16)
            values = jnp.concatenate([projected[rows, lanes(2)], ones], axis=1)
            sums = matmul(expo, values)
            heads = jnp.where(first_head, sums[:CELLS, :128], sums[CELLS:, :128]) / jnp.where(
                first_head, sums[:CELLS, 128:], sums[CELLS:, 128:]
            )
            attended[pl.ds(band * WH, WH), w * WL : (w + 1) * WL, lanes(0)] = heads.reshape(
                WH, WL, 128
            )

    loads["qkv"].wait()
    attend(1)
    copies.arrived("halo e", halo.at[0], east)
    copies.arrived("halo w", halo.at[1], west)

    @pl.loop(0, ROWS)
    def _(r):
        wide[r, 0:WL, :] = halo[0, r].astype(F32)
        wide[r, WL + COLS :, :] = halo[1, r].astype(F32)

    copies.start("inner1", inner_hbm.at[late], inner_ref.at[1, late], across)
    attend(0)
    attend(2)
    copies.start("outer", outer_hbm, outer_ref.at[other], across)

    loads["mix"].wait()

    @pl.loop(0, ROWS, unroll=4)
    def _(r):
        shifted[r] = pltpu.roll(attended[r], COLS + offset, 0)[:COLS].astype(BF16)

    @pl.loop(0, 2)
    def _(i):
        rows = pl.ds(i * 8, 8)
        mixed = matmul(shifted[rows].reshape(2 * CELLS, D1), mix_ref[...]).reshape(8, COLS, D1)
        mixed = (base[rows] + mixed).astype(BF16).astype(F32).reshape(4, 2, COLS, D1)
        for c in range(4):
            level[pl.ds(i * 4, 4), :, c] = mixed[..., c * 128 : (c + 1) * 128]

    def store_merged(r, quads):
        centre = sum(jnp.sum(quad, axis=1, keepdims=True) for quad in quads) / (4 * D1)
        quads = [quad - centre for quad in quads]
        spread = sum(jnp.sum(quad * quad, axis=1, keepdims=True) for quad in quads) / (4 * D1)
        scale = lax.rsqrt(spread + NORM_EPS)
        rows = pl.ds(pl.multiple_of(r * 16, 16), 16)
        for q in range(4):
            lanes = slice(q * D1, (q + 1) * D1)
            merged[rows, lanes] = (quads[q] * scale * merge_gain_ref[:, lanes]).astype(BF16)

    fold(store_merged)
    loads["merge"].wait()

    @pl.loop(0, 4)
    def _(j):
        lanes = pl.ds(pl.multiple_of(j * 256, 256), 256)
        coarse[:, lanes] = matmul(merged[...], merge_ref[:, lanes]).astype(BF16)

    @pl.loop(0, 4, unroll=4)
    def _(i):
        rows = pl.ds(pl.multiple_of(i * 32, 32), 32)
        lift[0, 0, rows, :] = (
            normalise(coarse[rows, :].astype(F32)) * coarse_gain_ref[...]
        ).astype(BF16)

    gather_lift.send("r0", 0, front, "r")
    gather_lift.send("l0", 0, rear, "l")
    gather_lift.send("r1", 0, rear, "r")
    gather_lift.send("l1", 0, front, "l")
    gather_lift.share(0)
    for way, dx in (("r", 3), ("l", 1), ("o", 2)):
        gather_cot.came(way, dx, None, way)
        gather_cot.share(dx)
    copies.arrived("inner0", inner_ref.at[1, early], across)
    copies.arrived("inner1", inner_ref.at[1, late], across)
    loads["inner"].wait()
    loads["outer"].wait()

    unit = lax.broadcasted_iota(jnp.int32, (256, 256), 0) == lax.broadcasted_iota(
        jnp.int32, (256, 256), 1
    )
    unit = jnp.where(unit, 1.0, 0.0).astype(BF16)

    def activate(dx):
        gather_lift.shared(dx)
        p = place(dx)
        columns = slice(p * 2 * CELLS, (p + 1) * 2 * CELLS)
        for half in range(2):
            rows = slice(half * 256, (half + 1) * 256)
            pre = matmul(lift[p].reshape(2 * CELLS, D2), inner_ref[half])
            value, slope = gelu_pair(pre)
            value = value.astype(BF16)
            hidden[p, :, rows] = value
            slopes[p, half] = slope
            hidden_t[rows, columns] = matmul_t(unit, value).astype(BF16)

    def project(dx):
        p = place(dx)
        part[p] = matmul(hidden[p], outer_ref[...]).astype(BF16).reshape(2, CELLS, D2)
        copies.start("s%d" % dx, part.at[p, 1], core_in.at[p], partner)

    def pull_back(half):
        rows = slice(half * 256, (half + 1) * 256)
        for p in range(4):
            columns = slice(p * 2 * CELLS, (p + 1) * 2 * CELLS)
            cot_hidden = matmul_t(cots[p].reshape(2 * CELLS, D2), outer_ref[rows, :])
            cot_pre = (cot_hidden * slopes[p, half]).astype(BF16)
            cot_pre_t[rows, columns] = matmul_t(unit, cot_pre).astype(BF16)

    def gradient(kind, half, begin, end):
        left_ref, array = ((cot_pre_t, lift), (hidden_t, cots))[kind]
        rows = slice(half * 256, (half + 1) * 256)

        @pl.loop(0, 4)
        def _(j):
            lanes = pl.ds(pl.multiple_of(j * 256, 256), 256)
            cells = array[begin:end, :, :, lanes].reshape((end - begin) * 2 * CELLS, 256)
            term = matmul(left_ref[rows, begin * 2 * CELLS : end * 2 * CELLS], cells)
            if begin > 0:
                term = term + sums[rows, lanes]
            if end < 4:
                sums[rows, lanes] = term
            else:
                for k in range(2):
                    terms[2 * j + k, kind, half] = term[:, k * 128 : (k + 1) * 128].astype(BF16)

    def cores(dx):
        p = place(dx)
        copies.arrived("s%d" % dx, core_in.at[p], partner)
        part[p, 0] = (part[p, 0].astype(F32) + core_in[p].astype(F32)).astype(BF16)
        if dx > 0:
            device = {1: right, 3: left, 2: opposite}[dx]
            copies.start("t%d" % dx, part.at[p, 0], x_in.at[dx - 1], device)

    def zed(dz):
        return (z + dz) % 8

    ways = ((0, up, 1), (1, down, -1))
    thin = (pl.ds(0, 128), pl.ds(128, 128))

    def term_of(mine, chain):
        if chain < 2:
            return terms.at[mine, 1, chain]
        return terms.at[mine, 0, 0, thin[chain - 2]]

    def landing(step, way, chain):
        if chain < 2:
            return ring_in.at[step, way, 0, chain]
        return ring_in.at[step, way, 1, 0, thin[chain - 2]]

    def ring_send(step, way, chain):
        device, sign = ways[way][1:]
        mine = zed(sign * (4 - step) + 8)
        name = "z%d%d%d" % (step, way, chain)
        copies.start(name, term_of(mine, chain), landing(step, way, chain), device)

    def ring_begin(chain):
        ring_send(0, chain % 2, chain)

    def ring_other(chain):
        ring_send(1, 1 - chain % 2, chain)

    def ring_take(step, way, chain):
        here = landing(step, way, chain)
        copies.arrived("z%d%d%d" % (step, way, chain), here, ways[way][1])
        return here[...].astype(F32)

    def ring_step(step, chain):
        for way, device, sign in ways:
            if step == 1 and way != chain % 2:
                continue
            mine = term_of(zed(sign * (4 - step) + 8), chain)
            mine[...] = (mine[...].astype(F32) + ring_take(step - 1, way, chain)).astype(BF16)
            ring_send(step, way, chain)

    def ring_end(chain):
        total = term_of(z, chain)[...].astype(F32)
        return total + ring_take(3, 0, chain) + ring_take(3, 1, chain)

    order = (4, 3, 5, 2, 6, 1, 7, 0)

    def pair_send(d):
        copies.start("y%d" % d, terms.at[zed(d), 0, 1], y_in.at[d], across)

    def pair_add(d):
        copies.arrived("y%d" % d, y_in.at[d], across)
        later = order.index(d) + 4
        if later < 8:
            pair_send(order[later])
        mine = zed(d)
        terms[mine, 0, 0] = (terms[mine, 0, 0].astype(F32) + y_in[d].astype(F32)).astype(BF16)

    def side_begin(total):
        side_out[0] = total.T.reshape(2, HALF, 256)
        side_in[1] = side_out[0, 1 - y_lo].astype(BF16)
        copies.start("side", side_in.at[1], side_in.at[0], side)

    corners = ((0, 1, side), (1, 0, across), (1, 1, corner))

    def corners_begin():
        totals = [ring_end(0), ring_end(1)]
        for half in range(2):
            side_out[1 + half] = totals[half].T.reshape(2, HALF, 256)
        for k, (half, turn, device) in enumerate(corners):
            row = 1 - y_lo if turn else y_lo
            corner_out[k] = side_out[1 + half, row].astype(BF16)
            copies.start("corner%d" % k, corner_out.at[k], corner_in.at[k], device)

    activate(0)
    for name, rows, dx, way in (("r0", front, 3, "r"), ("l0", rear, 1, "l")):
        gather_lift.came(name, dx, rows, way)
        gather_lift.send("f" + way, dx, rows, way)
    gather_lift.came("r1", 3, rear, "r")
    gather_lift.share(3)
    gather_lift.came("l1", 1, front, "l")
    gather_lift.share(1)
    activate(3)
    activate(1)
    for dx in (0, 3, 1, 2):
        gather_cot.shared(dx)
    gradient(1, 0, 0, 3)
    gradient(1, 1, 0, 3)
    gather_lift.came("fr", 2, front, "r")
    gather_lift.came("fl", 2, rear, "l")
    gather_lift.share(2)
    activate(2)
    gradient(1, 0, 3, 4)
    ring_begin(0)
    ring_other(0)
    gradient(1, 1, 3, 4)
    ring_begin(1)
    ring_other(1)
    copies.arrived("outer", outer_ref.at[other], across)
    pull_back(1)
    gradient(0, 1, 0, 4)
    for d in order[:4]:
        pair_send(d)
    ring_step(1, 0)
    ring_step(1, 1)
    project(2)
    project(3)
    project(1)
    project(0)
    cores(2)
    cores(3)
    cores(1)
    ring_step(2, 0)
    ring_step(2, 1)
    pull_back(0)
    gradient(0, 0, 0, 4)
    cores(0)
    pair_add(4)
    ring_begin(2)
    ring_begin(3)
    pair_add(3)
    pair_add(5)
    ring_other(2)
    ring_other(3)
    ring_step(3, 0)
    ring_step(3, 1)
    ring_step(1, 2)
    ring_step(1, 3)
    pair_add(2)
    pair_add(6)
    ring_step(2, 2)
    ring_step(2, 3)
    corners_begin()
    pair_add(1)
    pair_add(7)
    ring_step(3, 2)
    ring_step(3, 3)
    pair_add(0)

    update = part[0, 0].astype(F32)
    for dx, device in ((1, right), (3, left), (2, opposite)):
        copies.arrived("t%d" % dx, x_in.at[dx - 1], device)
        update = update + x_in[dx - 1].astype(F32)
    back[...] = (coarse[...].astype(F32) + update).astype(BF16)

    for q in range(4):
        raised = matmul(back[...], expand_ref[:, q * D1 : (q + 1) * D1])
        cells = pl.ds(q % 2, COLS // 2, stride=2)
        for c in range(4):
            block = raised[:, c * 128 : (c + 1) * 128].reshape(ROWS // 2, COLS // 2, 128)
            level[:, q // 2, c, cells, :] = level[:, q // 2, c, cells, :] + block

    @pl.loop(0, ROWS // 2)
    def _(r):
        for i in range(2):
            for c in range(4):
                prediction_ref[2 * r + i, :, c * 128 : (c + 1) * 128] = level[r, i, c].astype(BF16)

    side_begin(jnp.concatenate([ring_end(2), ring_end(3)], axis=0))
    total = side_out[1, y_lo]
    for k, (half, turn, device) in enumerate(corners):
        copies.arrived("corner%d" % k, corner_in.at[k], device)
        total = total + corner_in[k].astype(F32)
    grad_outer_ref[...] = total
    copies.arrived("side", side_in.at[0], side)
    grad_inner_ref[...] = side_out[0, y_lo] + side_in[0].astype(F32)
    copies.finish()


def hand_over_kernel(*refs):
    for k in range(3):
        refs[3 + k][...] = refs[k][...]


def local(
    features, land_mask, land_embed, window_shift, fine_gain, qkv_weight, bias_table, mix_weight,
    merge_gain, merge_weight, coarse_gain, inner_weight, outer_weight, expand_weight, cotangent,
):
    vmem = pl.BlockSpec(memory_space=pltpu.VMEM)
    smem = pl.BlockSpec(memory_space=pltpu.SMEM)
    anywhere = pl.BlockSpec(memory_space=pl.ANY)
    wide_block = pltpu.VMEM((4, 2, CELLS, D2), BF16)
    outputs = pl.pallas_call(
        window_kernel,
        out_shape=(
            jax.ShapeDtypeStruct((ROWS, COLS, D1), BF16),
            jax.ShapeDtypeStruct((HALF, 256), F32),
            jax.ShapeDtypeStruct((HALF, 256), F32),
        ),
        in_specs=[smem] + [vmem] * 6 + [anywhere] * 8,
        out_specs=(vmem,) * 3,
        scratch_shapes=[
            pltpu.VMEM((ROWS, COLS, D1), BF16),
            pltpu.VMEM((ROWS, COLS, D1), BF16),
            pltpu.VMEM((D1, 3 * D1), BF16),
            pltpu.VMEM((D1, D1), BF16),
            pltpu.VMEM((4 * D1, D2), BF16),
            pltpu.VMEM((2, D2, HIDDEN // 2), BF16),
            pltpu.VMEM((HIDDEN, D2), BF16),
            pltpu.VMEM((D2, 4 * D1), BF16),
            pltpu.VMEM((HEADS1, 512), F32),
            pltpu.VMEM((2 * WH - 1, HEADS1, 128), F32),
            pltpu.VMEM((ROWS, COLS, D1), F32),
            pltpu.VMEM((ROWS, COLS, D1), BF16),
            pltpu.VMEM((2, ROWS, WL, D1), BF16),
            pltpu.VMEM((ROWS, COLS + 2 * WL, D1), F32),
            pltpu.VMEM((HEADS1, CELLS, CELLS), F32),
            pltpu.VMEM((ROWS, WL, D1), BF16),
            pltpu.VMEM((ROWS * WL, 3 * D1), BF16),
            pltpu.VMEM((ROWS, COLS + WL, D1), F32),
            pltpu.VMEM((ROWS, COLS, D1), BF16),
            pltpu.VMEM((ROWS // 2, 2, 4, COLS, 128), F32),
            pltpu.VMEM((CELLS, 4 * D1), BF16),
            pltpu.VMEM((CELLS, D2), BF16),
            pltpu.VMEM((CELLS, D2), BF16),
            wide_block,
            wide_block,
            wide_block,
            pltpu.VMEM((4, CELLS, D2), BF16),
            pltpu.VMEM((3, CELLS, D2), BF16),
            pltpu.VMEM((4, 2 * CELLS, HIDDEN), BF16),
            pltpu.VMEM((4, 2, 2 * CELLS, 256), F32),
            pltpu.VMEM((HIDDEN, 8 * CELLS), BF16),
            pltpu.VMEM((HIDDEN, 8 * CELLS), BF16),
            pltpu.VMEM((HIDDEN, D2), F32),
            pltpu.VMEM((8, 2, 2, 256, 128), BF16),
            pltpu.VMEM((8, 256, 128), BF16),
            pltpu.VMEM((4, 2, 2, 2, 256, 128), BF16),
            pltpu.VMEM((3, 2, HALF, 256), F32),
            pltpu.VMEM((2, HALF, 256), BF16),
            pltpu.VMEM((3, HALF, 256), BF16),
            pltpu.VMEM((3, HALF, 256), BF16),
            pltpu.SemaphoreType.DMA((12,)),
            pltpu.SemaphoreType.DMA((COPIES,)),
            pltpu.SemaphoreType.DMA((COPIES,)),
        ],
        compiler_params=pltpu.CompilerParams(
            collective_id=0, has_side_effects=True, vmem_limit_bytes=56 * 1024 * 1024
        ),
        name="window",
    )(
        window_shift, land_mask, land_embed[None], fine_gain[None], bias_table,
        merge_gain[None], coarse_gain[None], features, cotangent,
        qkv_weight, mix_weight, merge_weight, inner_weight, outer_weight, expand_weight,
    )
    prediction, grad_inner, grad_outer = pl.pallas_call(
        hand_over_kernel,
        out_shape=tuple(jax.ShapeDtypeStruct(x.shape, x.dtype) for x in outputs),
        in_specs=[vmem] * 3,
        out_specs=(vmem,) * 3,
        name="hand_over",
    )(*outputs)
    return prediction, grad_inner, grad_outer.T


def solution(mesh):
    return jax.shard_map(
        local,
        mesh=mesh,
        in_specs=(
            P("lat", "lon", None),
            P("lat", "lon"),
            P(),
            P(),
            P(),
            P(),
            P(),
            P(),
            P(),
            P(),
            P(),
            P(None, "lon"),
            P("lon", None),
            P(),
            P("lat", "lon", None),
        ),
        out_specs=(P("lat", "lon", None), P("lat", "lon"), P("lon", "lat")),
        check_vma=False,
    )
```

```python
import jax
import jax.numpy as jnp
from jax import lax
from jax.experimental import pallas as pl
from jax.experimental.pallas import tpu as pltpu
from jax.sharding import PartitionSpec as P

HEADS1 = 8
WH = 8
WL = 16
D1 = 512
D2 = 1024
ROWS = 16
COLS = 32
CELLS = 128
HALF = 64
COPIES = 72
HIDDEN = 512

NORM_EPS = 1e-05
GELU_SCALE = 0.7978845608028654
MESH = pl.DeviceIdType.MESH
BF16 = jnp.bfloat16
F32 = jnp.float32
LAST = (((1,), (1,)), ((), ()))


def normalise(values):
    centre = jnp.mean(values, axis=-1, keepdims=True)
    centred = values - centre
    spread = jnp.mean(centred * centred, axis=-1, keepdims=True)
    return centred * lax.rsqrt(spread + NORM_EPS)


def gelu_pair(pre_act):
    square = pre_act * pre_act
    inner = GELU_SCALE * (pre_act + 0.044715 * square * pre_act)
    tangent = jnp.tanh(inner)
    half = 0.5 * (1.0 + tangent)
    value = pre_act * half
    slope = half + value * (1.0 - tangent) * (GELU_SCALE + (3.0 * 0.044715 * GELU_SCALE) * square)
    return (value, slope)


def matmul(a, b):
    return jnp.dot(a, b, preferred_element_type=F32)


def matmul_t(a, b):
    return lax.dot_general(a, b, LAST, preferred_element_type=F32)


class Copies:
    def __init__(self, send_sems, recv_sems):
        self.send_sems, self.recv_sems = send_sems, recv_sems
        self.places, self.started = {}, []

    def describe(self, name, src, dst, device):
        place = self.places.setdefault(name, len(self.places))
        return pltpu.make_async_remote_copy(
            src_ref=src,
            dst_ref=dst,
            send_sem=self.send_sems.at[place],
            recv_sem=self.recv_sems.at[place],
            device_id=device,
            device_id_type=MESH,
        )

    def start(self, name, src, dst, device):
        copy = self.describe(name, src, dst, device)
        copy.start()
        self.started.append(copy)

    def arrived(self, name, dst, device):
        self.describe(name, dst, dst, device).wait_recv()

    def finish(self):
        for copy in self.started:
            copy.wait_send()


def window_kernel(
    shift_ref, mask_ref, embed_ref, fine_gain_ref, table_ref, merge_gain_ref,
    coarse_gain_ref,
    features_hbm, cotangent_hbm, qkv_hbm, mix_hbm, merge_hbm, inner_hbm, outer_hbm, expand_hbm,
    prediction_ref, grad_inner_ref, grad_outer_ref,
    features_ref, cotangent_ref, qkv_ref, mix_ref, merge_ref, inner_ref, outer_ref, expand_ref,
    padded, table_rows, base, normed, halo, wide, bias, window, projected, attended, shifted, level, merged, coarse, back,
    lift, cots, part, core_in, x_in,
    hidden, slopes, hidden_t, cot_pre_t, sums, terms, y_in, ring_in, side_out, side_in, corner_out, corner_in,
    load_sems, send_sems, recv_sems,
):
    lon, lat = lax.axis_index("lon"), lax.axis_index("lat")
    core, y_hi, x = lon % 2, (lon // 2) % 2, lon // 4
    z, y_lo = lat // 2, lat % 2
    east, west = {"lon": (lon + 1) % 16}, {"lon": (lon + 15) % 16}
    partner = {"lon": lon + 1 - 2 * core}
    across = {"lon": lon + 2 - 4 * y_hi}
    right, left = {"lon": (lon + 4) % 16}, {"lon": (lon + 12) % 16}
    opposite = {"lon": (lon + 8) % 16}
    up, down = {"lat": (lat + 2) % 16}, {"lat": (lat + 14) % 16}
    side = {"lat": lat + 1 - 2 * y_lo}
    corner = {"lat": lat + 1 - 2 * y_lo, "lon": lon + 2 - 4 * y_hi}

    loads, slots = {}, iter(range(12))

    def load(name, src, dst):
        loads[name] = pltpu.make_async_copy(src, dst, load_sems.at[next(slots)])
        loads[name].start()

    own = pl.ds(0, HIDDEN // 2)
    other = pl.ds(HIDDEN // 2, HIDDEN // 2)
    load("features", features_hbm, features_ref)
    load("cotangent", cotangent_hbm, cotangent_ref)
    for j in range(4):
        rows = pl.ds(j * 256, 256)
        load("expand%d" % j, expand_hbm.at[rows], expand_ref.at[rows])
    barrier = pltpu.get_barrier_semaphore()
    neighbours = (east, west, partner, across, right, left, opposite, up, down, side, corner)
    for device in neighbours:
        pl.semaphore_signal(barrier, inc=1, device_id=device, device_id_type=MESH)

    loads["features"].wait()
    pl.semaphore_wait(barrier, len(neighbours))
    copies = Copies(send_sems, recv_sems)
    early, late = pl.ds(0, 256), pl.ds(256, D2 - 256)
    copies.start("inner0", inner_hbm.at[early], inner_ref.at[1, early], across)

    diagonal = lax.broadcasted_iota(jnp.int32, (COLS, COLS), 0) == lax.broadcasted_iota(
        jnp.int32, (COLS, COLS), 1
    )

    @pl.loop(0, ROWS, unroll=4)
    def _(r):
        land = mask_ref[pl.ds(r, 1), :].astype(F32)
        land = jnp.sum(jnp.where(diagonal, land, 0.0), axis=1, keepdims=True)
        cells = features_ref[r].astype(F32) + land * embed_ref[...]
        base[r] = cells
        rounded = (normalise(cells) * fine_gain_ref[...]).astype(BF16)
        normed[r] = rounded
        wide[r, WL : WL + COLS, :] = rounded.astype(F32)

    copies.start("halo e", normed.at[:, pl.ds(COLS - WL, WL), :], halo.at[0], east)
    copies.start("halo w", normed.at[:, pl.ds(0, WL), :], halo.at[1], west)

    padded[...] = jnp.zeros_like(padded)
    padded[:, 0 : table_ref.shape[1]] = table_ref[...]
    offsets = padded[...]
    top = offsets.astype(BF16)
    rest = offsets - top.astype(F32)
    middle = rest.astype(BF16)
    bottom = (rest - middle.astype(F32)).astype(BF16)
    turn = lax.broadcasted_iota(jnp.int32, (512, 640), 0) + lax.broadcasted_iota(
        jnp.int32, (512, 640), 1
    )
    turn = jnp.where(turn == table_ref.shape[1] - 1, 1.0, 0.0).astype(BF16)
    flipped = matmul(top, turn) + matmul(middle, turn) + matmul(bottom, turn)
    for i in range(2 * WH - 1):
        start = i * (2 * WL - 1)
        table_rows[i] = flipped[:, start : start + 128]
    lane = lax.broadcasted_iota(jnp.int32, (WL, 128), 1)

    @pl.loop(0, HEADS1, unroll=4)
    def _(h):
        halves = []
        for k in range(2):
            total = jnp.zeros((WL, 128), F32)
            for i in range(8 if k == 0 else 7):
                row = jnp.broadcast_to(table_rows[8 * k + i, pl.ds(h, 1), :], (WL, 128))
                turned = pltpu.roll(row, (128 - 15 + 16 * i) % 128, 1, stride=1, stride_axis=0)
                total = jnp.where(lane // 16 == i, turned, total)
            halves.append(total)
        both = jnp.concatenate(halves, axis=1)
        for i in range(WH):
            start = (WH - 1 - i) * WL
            bias[h, i * WL : (i + 1) * WL, :] = both[:, start : start + 128]

    def place(dx):
        return (0, 1, 3, 2)[dx % 4]

    def fold(store):
        @pl.loop(0, ROWS // 2, unroll=4)
        def _(r):
            store(
                r,
                [
                    jnp.concatenate(
                        [level[r, i, c, pl.ds(j, COLS // 2, stride=2), :] for c in range(4)], axis=1
                    )
                    for i in range(2)
                    for j in range(2)
                ],
            )

    loads["cotangent"].wait()

    @pl.loop(0, ROWS // 2)
    def _(r):
        for i in range(2):
            cells = cotangent_ref[2 * r + i].astype(F32)
            for c in range(4):
                level[r, i, c] = cells[:, c * 128 : (c + 1) * 128]

    def store_cot(r, quads):
        rows = pl.ds(pl.multiple_of(r * 16, 16), 16)
        for q in range(4):
            merged[rows, q * D1 : (q + 1) * D1] = quads[q].astype(BF16)

    fold(store_cot)
    for j in range(4):
        lanes = slice(j * 256, (j + 1) * 256)
        loads["expand%d" % j].wait()
        if j == 2:
            load("qkv", qkv_hbm, qkv_ref)
        cots[0, 0, :, lanes] = matmul_t(merged[...], expand_ref[lanes, :]).astype(BF16)

    load("mix", mix_hbm, mix_ref)
    load("merge", merge_hbm, merge_ref)
    load("inner", inner_hbm, inner_ref.at[0])
    load("outer", outer_hbm, outer_ref.at[own])

    front, rear = pl.ds(0, HALF), pl.ds(HALF, HALF)
    moves = {"r": (right, -1, 0), "l": (left, 1, 0), "o": (opposite, 2, 0), "p": (partner, 0, 1)}

    class Gather:
        def __init__(self, name, array):
            self.name, self.array = name, array

        def at(self, dx, rows=None, dk=0):
            block = self.array.at[place(dx), dk]
            return block if rows is None else block.at[rows]

        def send(self, name, dx, rows, way):
            device, mx, mk = moves[way]
            copies.start(self.name + name, self.at(dx, rows), self.at(dx + mx, rows, mk), device)

        def came(self, name, dx, rows, way):
            copies.arrived(self.name + name, self.at(dx, rows), moves[way][0])

        def share(self, dx):
            self.send("p%d" % dx, dx, None, "p")

        def shared(self, dx):
            copies.arrived(self.name + "p%d" % dx, self.at(dx, None, 1), partner)

    gather_cot, gather_lift = Gather("c", cots), Gather("l", lift)
    gather_cot.send("r", 0, None, "r")
    gather_cot.send("l", 0, None, "l")
    gather_cot.send("o", 0, None, "o")
    gather_cot.share(0)

    offset = shift_ref[0]
    first_head = lax.broadcasted_iota(jnp.int32, (CELLS, 128), 1) < 64
    ones = jnp.ones((CELLS, 128), BF16)

    def attend(w):
        @pl.loop(0, ROWS, unroll=4)
        def _(r):
            cells = wide[r, w * WL : (w + 2) * WL, :]
            window[r] = pltpu.roll(cells, 2 * WL - offset, 0)[:WL].astype(BF16)

        @pl.loop(0, 6, unroll=3)
        def _(j):
            lanes = pl.ds(pl.multiple_of(j * 256, 256), 256)
            rows = window[...].reshape(ROWS * WL, D1)
            projected[:, lanes] = matmul(rows, qkv_ref[:, lanes]).astype(BF16)

        @pl.loop(0, 8, unroll=8)
        def _(k):
            band, pair = k // 4, k % 4
            rows = pl.ds(pl.multiple_of(band * CELLS, CELLS), CELLS)

            def lanes(kind):
                return pl.ds(pl.multiple_of(kind * D1 + pair * 128, 128), 128)

            queries = projected[rows, lanes(0)] * 0.125
            zero = jnp.zeros_like(queries)
            queries = jnp.concatenate(
                [jnp.where(first_head, queries, zero), jnp.where(first_head, zero, queries)], axis=0
            )
            scores = matmul_t(queries, projected[rows, lanes(1)])
            scores = scores + bias[pl.ds(2 * pair, 2)].reshape(2 * CELLS, 128)
            expo = jnp.exp(scores - jnp.max(scores, axis=1, keepdims=True)).astype(BF16)
            values = jnp.concatenate([projected[rows, lanes(2)], ones], axis=1)
            sums = matmul(expo, values)
            heads = jnp.where(first_head, sums[:CELLS, :128], sums[CELLS:, :128]) / jnp.where(
                first_head, sums[:CELLS, 128:], sums[CELLS:, 128:]
            )
            attended[pl.ds(band * WH, WH), w * WL : (w + 1) * WL, lanes(0)] = heads.reshape(
                WH, WL, 128
            )

    loads["qkv"].wait()
    attend(1)
    copies.arrived("halo e", halo.at[0], east)
    copies.arrived("halo w", halo.at[1], west)

    @pl.loop(0, ROWS, unroll=4)
    def _(r):
        wide[r, 0:WL, :] = halo[0, r].astype(F32)
        wide[r, WL + COLS :, :] = halo[1, r].astype(F32)

    copies.start("inner1", inner_hbm.at[late], inner_ref.at[1, late], across)
    attend(0)
    attend(2)
    copies.start("outer", outer_hbm, outer_ref.at[other], across)

    loads["mix"].wait()

    @pl.loop(0, ROWS, unroll=4)
    def _(r):
        shifted[r] = pltpu.roll(attended[r], COLS + offset, 0)[:COLS].astype(BF16)

    @pl.loop(0, 2, unroll=2)
    def _(i):
        rows = pl.ds(i * 8, 8)
        mixed = matmul(shifted[rows].reshape(2 * CELLS, D1), mix_ref[...]).reshape(8, COLS, D1)
        mixed = (base[rows] + mixed).astype(BF16).astype(F32).reshape(4, 2, COLS, D1)
        for c in range(4):
            level[pl.ds(i * 4, 4), :, c] = mixed[..., c * 128 : (c + 1) * 128]

    def store_merged(r, quads):
        centre = sum(jnp.sum(quad, axis=1, keepdims=True) for quad in quads) / (4 * D1)
        quads = [quad - centre for quad in quads]
        spread = sum(jnp.sum(quad * quad, axis=1, keepdims=True) for quad in quads) / (4 * D1)
        scale = lax.rsqrt(spread + NORM_EPS)
        rows = pl.ds(pl.multiple_of(r * 16, 16), 16)
        for q in range(4):
            lanes = slice(q * D1, (q + 1) * D1)
            merged[rows, lanes] = (quads[q] * scale * merge_gain_ref[:, lanes]).astype(BF16)

    fold(store_merged)
    loads["merge"].wait()

    @pl.loop(0, 4, unroll=4)
    def _(j):
        lanes = pl.ds(pl.multiple_of(j * 256, 256), 256)
        coarse[:, lanes] = matmul(merged[...], merge_ref[:, lanes]).astype(BF16)

    @pl.loop(0, 4, unroll=4)
    def _(i):
        rows = pl.ds(pl.multiple_of(i * 32, 32), 32)
        lift[0, 0, rows, :] = (
            normalise(coarse[rows, :].astype(F32)) * coarse_gain_ref[...]
        ).astype(BF16)

    gather_lift.send("r0", 0, front, "r")
    gather_lift.send("l0", 0, rear, "l")
    gather_lift.send("r1", 0, rear, "r")
    gather_lift.send("l1", 0, front, "l")
    gather_lift.share(0)
    for way, dx in (("r", 3), ("l", 1), ("o", 2)):
        gather_cot.came(way, dx, None, way)
        gather_cot.share(dx)
    copies.arrived("inner0", inner_ref.at[1, early], across)
    copies.arrived("inner1", inner_ref.at[1, late], across)
    loads["inner"].wait()
    loads["outer"].wait()

    unit = lax.broadcasted_iota(jnp.int32, (256, 256), 0) == lax.broadcasted_iota(
        jnp.int32, (256, 256), 1
    )
    unit = jnp.where(unit, 1.0, 0.0).astype(BF16)

    def activate(dx):
        gather_lift.shared(dx)
        p = place(dx)
        columns = slice(p * 2 * CELLS, (p + 1) * 2 * CELLS)
        for half in range(2):
            rows = slice(half * 256, (half + 1) * 256)
            pre = matmul(lift[p].reshape(2 * CELLS, D2), inner_ref[half])
            value, slope = gelu_pair(pre)
            value = value.astype(BF16)
            hidden[p, :, rows] = value
            slopes[p, half] = slope
            hidden_t[rows, columns] = matmul_t(unit, value).astype(BF16)

    def project(dx):
        p = place(dx)
        part[p] = matmul(hidden[p], outer_ref[...]).astype(BF16).reshape(2, CELLS, D2)
        copies.start("s%d" % dx, part.at[p, 1], core_in.at[p], partner)

    def pull_back(half):
        rows = slice(half * 256, (half + 1) * 256)
        for p in range(4):
            columns = slice(p * 2 * CELLS, (p + 1) * 2 * CELLS)
            cot_hidden = matmul_t(cots[p].reshape(2 * CELLS, D2), outer_ref[rows, :])
            cot_pre = (cot_hidden * slopes[p, half]).astype(BF16)
            cot_pre_t[rows, columns] = matmul_t(unit, cot_pre).astype(BF16)

    def gradient(kind, half, begin, end):
        left_ref, array = ((cot_pre_t, lift), (hidden_t, cots))[kind]
        rows = slice(half * 256, (half + 1) * 256)

        @pl.loop(0, 4, unroll=4)
        def _(j):
            lanes = pl.ds(pl.multiple_of(j * 256, 256), 256)
            cells = array[begin:end, :, :, lanes].reshape((end - begin) * 2 * CELLS, 256)
            term = matmul(left_ref[rows, begin * 2 * CELLS : end * 2 * CELLS], cells)
            if begin > 0:
                term = term + sums[rows, lanes]
            if end < 4:
                sums[rows, lanes] = term
            else:
                for k in range(2):
                    terms[2 * j + k, kind, half] = term[:, k * 128 : (k + 1) * 128].astype(BF16)

    def cores(dx):
        p = place(dx)
        copies.arrived("s%d" % dx, core_in.at[p], partner)
        part[p, 0] = (part[p, 0].astype(F32) + core_in[p].astype(F32)).astype(BF16)
        if dx > 0:
            device = {1: right, 3: left, 2: opposite}[dx]
            copies.start("t%d" % dx, part.at[p, 0], x_in.at[dx - 1], device)

    def zed(dz):
        return (z + dz) % 8

    ways = ((0, up, 1), (1, down, -1))
    thin = (pl.ds(0, 128), pl.ds(128, 128))

    def term_of(mine, chain):
        if chain < 2:
            return terms.at[mine, 1, chain]
        return terms.at[mine, 0, 0, thin[chain - 2]]

    def landing(step, way, chain):
        if chain < 2:
            return ring_in.at[step, way, 0, chain]
        return ring_in.at[step, way, 1, 0, thin[chain - 2]]

    def ring_send(step, way, chain):
        device, sign = ways[way][1:]
        mine = zed(sign * (4 - step) + 8)
        name = "z%d%d%d" % (step, way, chain)
        copies.start(name, term_of(mine, chain), landing(step, way, chain), device)

    def ring_begin(chain):
        ring_send(0, chain % 2, chain)

    def ring_other(chain):
        ring_send(1, 1 - chain % 2, chain)

    def ring_take(step, way, chain):
        here = landing(step, way, chain)
        copies.arrived("z%d%d%d" % (step, way, chain), here, ways[way][1])
        return here[...].astype(F32)

    def ring_step(step, chain):
        for way, device, sign in ways:
            if step == 1 and way != chain % 2:
                continue
            mine = term_of(zed(sign * (4 - step) + 8), chain)
            mine[...] = (mine[...].astype(F32) + ring_take(step - 1, way, chain)).astype(BF16)
            ring_send(step, way, chain)

    def ring_end(chain):
        total = term_of(z, chain)[...].astype(F32)
        return total + ring_take(3, 0, chain) + ring_take(3, 1, chain)

    order = (4, 3, 5, 2, 6, 1, 7, 0)

    def pair_send(d):
        copies.start("y%d" % d, terms.at[zed(d), 0, 1], y_in.at[d], across)

    def pair_add(d):
        copies.arrived("y%d" % d, y_in.at[d], across)
        later = order.index(d) + 4
        if later < 8:
            pair_send(order[later])
        mine = zed(d)
        terms[mine, 0, 0] = (terms[mine, 0, 0].astype(F32) + y_in[d].astype(F32)).astype(BF16)

    def side_begin(total):
        side_out[0] = total.T.reshape(2, HALF, 256)
        side_in[1] = side_out[0, 1 - y_lo].astype(BF16)
        copies.start("side", side_in.at[1], side_in.at[0], side)

    corners = ((0, 1, side), (1, 0, across), (1, 1, corner))

    def corners_begin():
        totals = [ring_end(0), ring_end(1)]
        for half in range(2):
            side_out[1 + half] = totals[half].T.reshape(2, HALF, 256)
        for k, (half, turn, device) in enumerate(corners):
            row = 1 - y_lo if turn else y_lo
            corner_out[k] = side_out[1 + half, row].astype(BF16)
            copies.start("corner%d" % k, corner_out.at[k], corner_in.at[k], device)

    activate(0)
    for name, rows, dx, way in (("r0", front, 3, "r"), ("l0", rear, 1, "l")):
        gather_lift.came(name, dx, rows, way)
        gather_lift.send("f" + way, dx, rows, way)
    gather_lift.came("r1", 3, rear, "r")
    gather_lift.share(3)
    gather_lift.came("l1", 1, front, "l")
    gather_lift.share(1)
    activate(3)
    activate(1)
    for dx in (0, 3, 1, 2):
        gather_cot.shared(dx)
    gradient(1, 0, 0, 3)
    gradient(1, 1, 0, 3)
    gather_lift.came("fr", 2, front, "r")
    gather_lift.came("fl", 2, rear, "l")
    gather_lift.share(2)
    activate(2)
    gradient(1, 0, 3, 4)
    ring_begin(0)
    ring_other(0)
    gradient(1, 1, 3, 4)
    ring_begin(1)
    ring_other(1)
    copies.arrived("outer", outer_ref.at[other], across)
    pull_back(1)
    gradient(0, 1, 0, 4)
    for d in order[:4]:
        pair_send(d)
    ring_step(1, 0)
    ring_step(1, 1)
    project(2)
    project(3)
    project(1)
    project(0)
    cores(2)
    cores(3)
    cores(1)
    ring_step(2, 0)
    ring_step(2, 1)
    pull_back(0)
    gradient(0, 0, 0, 4)
    cores(0)
    pair_add(4)
    ring_begin(2)
    ring_begin(3)
    pair_add(3)
    pair_add(5)
    ring_other(2)
    ring_other(3)
    ring_step(3, 0)
    ring_step(3, 1)
    ring_step(1, 2)
    ring_step(1, 3)
    pair_add(2)
    pair_add(6)
    ring_step(2, 2)
    ring_step(2, 3)
    corners_begin()
    pair_add(1)
    pair_add(7)
    ring_step(3, 2)
    ring_step(3, 3)
    pair_add(0)

    update = part[0, 0].astype(F32)
    for dx, device in ((1, right), (3, left), (2, opposite)):
        copies.arrived("t%d" % dx, x_in.at[dx - 1], device)
        update = update + x_in[dx - 1].astype(F32)
    back[...] = (coarse[...].astype(F32) + update).astype(BF16)

    for q in range(4):
        raised = matmul(back[...], expand_ref[:, q * D1 : (q + 1) * D1])
        cells = pl.ds(q % 2, COLS // 2, stride=2)
        for c in range(4):
            block = raised[:, c * 128 : (c + 1) * 128].reshape(ROWS // 2, COLS // 2, 128)
            level[:, q // 2, c, cells, :] = level[:, q // 2, c, cells, :] + block

    @pl.loop(0, ROWS // 2, unroll=4)
    def _(r):
        for i in range(2):
            for c in range(4):
                prediction_ref[2 * r + i, :, c * 128 : (c + 1) * 128] = level[r, i, c].astype(BF16)

    side_begin(jnp.concatenate([ring_end(2), ring_end(3)], axis=0))
    total = side_out[1, y_lo]
    for k, (half, turn, device) in enumerate(corners):
        copies.arrived("corner%d" % k, corner_in.at[k], device)
        total = total + corner_in[k].astype(F32)
    grad_outer_ref[...] = total
    copies.arrived("side", side_in.at[0], side)
    grad_inner_ref[...] = side_out[0, y_lo] + side_in[0].astype(F32)
    copies.finish()


def hand_over_kernel(*refs):
    for k in range(3):
        refs[3 + k][...] = refs[k][...]


def local(
    features, land_mask, land_embed, window_shift, fine_gain, qkv_weight, bias_table, mix_weight,
    merge_gain, merge_weight, coarse_gain, inner_weight, outer_weight, expand_weight, cotangent,
):
    vmem = pl.BlockSpec(memory_space=pltpu.VMEM)
    smem = pl.BlockSpec(memory_space=pltpu.SMEM)
    anywhere = pl.BlockSpec(memory_space=pl.ANY)
    wide_block = pltpu.VMEM((4, 2, CELLS, D2), BF16)
    outputs = pl.pallas_call(
        window_kernel,
        out_shape=(
            jax.ShapeDtypeStruct((ROWS, COLS, D1), BF16),
            jax.ShapeDtypeStruct((HALF, 256), F32),
            jax.ShapeDtypeStruct((HALF, 256), F32),
        ),
        in_specs=[smem] + [vmem] * 6 + [anywhere] * 8,
        out_specs=(vmem,) * 3,
        scratch_shapes=[
            pltpu.VMEM((ROWS, COLS, D1), BF16),
            pltpu.VMEM((ROWS, COLS, D1), BF16),
            pltpu.VMEM((D1, 3 * D1), BF16),
            pltpu.VMEM((D1, D1), BF16),
            pltpu.VMEM((4 * D1, D2), BF16),
            pltpu.VMEM((2, D2, HIDDEN // 2), BF16),
            pltpu.VMEM((HIDDEN, D2), BF16),
            pltpu.VMEM((D2, 4 * D1), BF16),
            pltpu.VMEM((HEADS1, 512), F32),
            pltpu.VMEM((2 * WH - 1, HEADS1, 128), F32),
            pltpu.VMEM((ROWS, COLS, D1), F32),
            pltpu.VMEM((ROWS, COLS, D1), BF16),
            pltpu.VMEM((2, ROWS, WL, D1), BF16),
            pltpu.VMEM((ROWS, COLS + 2 * WL, D1), F32),
            pltpu.VMEM((HEADS1, CELLS, CELLS), F32),
            pltpu.VMEM((ROWS, WL, D1), BF16),
            pltpu.VMEM((ROWS * WL, 3 * D1), BF16),
            pltpu.VMEM((ROWS, COLS + WL, D1), F32),
            pltpu.VMEM((ROWS, COLS, D1), BF16),
            pltpu.VMEM((ROWS // 2, 2, 4, COLS, 128), F32),
            pltpu.VMEM((CELLS, 4 * D1), BF16),
            pltpu.VMEM((CELLS, D2), BF16),
            pltpu.VMEM((CELLS, D2), BF16),
            wide_block,
            wide_block,
            wide_block,
            pltpu.VMEM((4, CELLS, D2), BF16),
            pltpu.VMEM((3, CELLS, D2), BF16),
            pltpu.VMEM((4, 2 * CELLS, HIDDEN), BF16),
            pltpu.VMEM((4, 2, 2 * CELLS, 256), F32),
            pltpu.VMEM((HIDDEN, 8 * CELLS), BF16),
            pltpu.VMEM((HIDDEN, 8 * CELLS), BF16),
            pltpu.VMEM((HIDDEN, D2), F32),
            pltpu.VMEM((8, 2, 2, 256, 128), BF16),
            pltpu.VMEM((8, 256, 128), BF16),
            pltpu.VMEM((4, 2, 2, 2, 256, 128), BF16),
            pltpu.VMEM((3, 2, HALF, 256), F32),
            pltpu.VMEM((2, HALF, 256), BF16),
            pltpu.VMEM((3, HALF, 256), BF16),
            pltpu.VMEM((3, HALF, 256), BF16),
            pltpu.SemaphoreType.DMA((12,)),
            pltpu.SemaphoreType.DMA((COPIES,)),
            pltpu.SemaphoreType.DMA((COPIES,)),
        ],
        compiler_params=pltpu.CompilerParams(
            collective_id=0, has_side_effects=True, vmem_limit_bytes=56 * 1024 * 1024
        ),
        name="window",
    )(
        window_shift, land_mask, land_embed[None], fine_gain[None], bias_table,
        merge_gain[None], coarse_gain[None], features, cotangent,
        qkv_weight, mix_weight, merge_weight, inner_weight, outer_weight, expand_weight,
    )
    prediction, grad_inner, grad_outer = pl.pallas_call(
        hand_over_kernel,
        out_shape=tuple(jax.ShapeDtypeStruct(x.shape, x.dtype) for x in outputs),
        in_specs=[vmem] * 3,
        out_specs=(vmem,) * 3,
        name="hand_over",
    )(*outputs)
    return prediction, grad_inner, grad_outer.T


def solution(mesh):
    return jax.shard_map(
        local,
        mesh=mesh,
        in_specs=(
            P("lat", "lon", None),
            P("lat", "lon"),
            P(),
            P(),
            P(),
            P(),
            P(),
            P(),
            P(),
            P(),
            P(),
            P(None, "lon"),
            P("lon", None),
            P(),
            P("lat", "lon", None),
        ),
        out_specs=(P("lat", "lon", None), P("lat", "lon"), P("lon", "lat")),
        check_vma=False,
    )
```
